128 devices in a mesh: dp: 64 (over z, y, x_hi, core), pipe: 2 (over x_lo).
Axes of the slice: x: 4 (x_hi: 2, x_lo: 2; x = x_hi * 2 + x_lo), y: 4, z: 4, core: 2. Of those that a mesh axis runs over, the one named last changes fastest.
Arguments:
- inputs: bfloat16 [81920, 4096], P(('pipe', 'dp')), parts along dimension 0, may hold values from -6 to 6
- out_grad: bfloat16 [81920, 4608], P(('pipe', 'dp')), parts along dimension 0, may hold values from -0.078125 to 0.078125
- a_inverse: bfloat16 [8192, 4096], P(('pipe', 'dp')), parts along dimension 0, may hold values from -1 to 2, as said below
- g_inverse: bfloat16 [9216, 4608], P(('pipe', 'dp')), parts along dimension 0, may hold values from -1 to 2, as said below
- weights: float32 [9216, 4096], P(('pipe', 'dp')), parts along dimension 0, may hold values from -6 to 6
- momentum: float32 [9216, 4096], P(('pipe', 'dp')), parts along dimension 0, may hold values from -6 to 6
Outputs:
- new_weights: float32 [9216, 4096], P(('pipe', 'dp')), parts along dimension 0
- new_momentum: float32 [9216, 4096], P(('pipe', 'dp')), parts along dimension 0
The draws below stay inside these ranges and needn't reach their ends.
There are 2 independent parts, one for each index of `pipe`. The reference program is written for one: setup_inputs(seed, part) draws one part's arguments, and reference() takes and returns one part's arrays. A program takes and returns all parts, laid end to end along the dimension named above; each array names one. Nothing has to cross between parts.
Inputs may be any that keep to these rules, and one draw needn't show every extreme that they name: a_inverse is symmetric and positive definite. g_inverse is symmetric and positive definite.
All inputs are finite; a program needn't handle non-finite values.
Results may differ from the reference program's by a relative error of at most 0.0037.
Values may be sent and summed in bfloat16 or wider, within the bound.
A program may use at most 320 MiB of HBM per device.

```python
import jax
import jax.numpy as jnp
from jax import lax

IN = 4096
OUT = 4608
TOKENS = 40960


def symmetric_from(noise, diag_values, width):
    shaped = (noise + noise.T) * (0.2 / jnp.sqrt(2.0 * width))
    eye_mask = (jnp.arange(width)[:, None] == jnp.arange(width)[None, :]).astype(jnp.float32)
    return (shaped * (1.0 - eye_mask) + eye_mask * diag_values[None, :]).astype(jnp.bfloat16)


def draw_a_inverse(key, part):
    key = jax.random.fold_in(key, 11)
    first, second = jax.random.split(key)
    noise = jax.random.normal(first, (IN, IN), jnp.float32)
    diag_values = jnp.exp(jax.random.uniform(second, (IN,), jnp.float32, -0.4, 0.4))
    return symmetric_from(noise, diag_values, IN)


def draw_g_inverse(key, part):
    key = jax.random.fold_in(key, 23)
    first, second = jax.random.split(key)
    noise = jax.random.normal(first, (OUT, OUT), jnp.float32)
    diag_values = jnp.exp(jax.random.uniform(second, (OUT,), jnp.float32, -0.4, 0.4))
    return symmetric_from(noise, diag_values, OUT)


def strengthened(result, own_key, source, target, parts, factor):
    def block_of(axis_at):
        return (jnp.arange(result.shape[axis_at]) // (result.shape[axis_at] // parts)).reshape((-1,) + (1,) * (result.ndim - 1 - axis_at))

    one_side = jax.random.permutation(own_key, parts)[block_of(target)]
    other_side = (block_of(target) + parts // 2) % parts
    return jnp.where((block_of(source) == one_side) | (block_of(source) == other_side), factor * result, result)


def level_of(stream_key, shape, shards, least, top_value):
    gain, own = 1.0, jax.random.fold_in(stream_key, 6)
    for dim, parts in shards:
        heights = jnp.exp(jax.random.uniform(jax.random.fold_in(own, dim), (parts,), jnp.float32, least / len(shards), top_value / len(shards)))
        gain = gain * jnp.repeat(heights, shape[dim] // parts).reshape([-1 if axis == dim else 1 for axis in range(len(shape))])
    return gain


def normal_values(rng, shape, scale, most, pieces=(), held_as=jnp.bfloat16):
    array = jax.random.normal(rng, shape, jnp.float32) * scale
    if len(pieces) > 0:
        array = level_of(rng, shape, pieces, -0.22, 0.18) * array
    return jnp.clip(array, min=-most, max=most).astype(held_as)


def bell_draw_with(key, shape, spread, bound, pieces, heavy, kind=jnp.bfloat16):
    result = spread * jax.random.normal(key, shape, jnp.float32)
    if pieces:
        result = result * level_of(key, shape, pieces, -0.22, 0.18)
    return jnp.clip(strengthened(result, jax.random.fold_in(key, 3), *heavy), -bound, bound).astype(kind)


def setup_inputs(seed: int = 0, part: int = 0) -> dict:
    keys = jax.random.split(jax.random.key(seed), 7)
    own_keys = jax.random.split(jax.random.fold_in(keys[6], part), 7)
    return {
        "inputs": normal_values(own_keys[0], (TOKENS, IN), 1.0, 6.0, ((0, 64),)),
        "out_grad": bell_draw_with(own_keys[1], (TOKENS, OUT), TOKENS ** -0.5, 0.078125, ((0, 64),), (0, 1, 64, 4.0)),
        "a_inverse": draw_a_inverse(jax.random.fold_in(jax.random.fold_in(keys[6], part), 71), part),
        "g_inverse": draw_g_inverse(jax.random.fold_in(jax.random.fold_in(keys[6], part), 71), part),
        "weights": normal_values(own_keys[4], (OUT, IN), 1.0, 6.0, ((0, 64),), jnp.float32),
        "momentum": normal_values(own_keys[5], (OUT, IN), 1.0, 6.0, ((0, 64),), jnp.float32),
    }


def reference(inputs, out_grad, a_inverse, g_inverse, weights, momentum):
    gradient = lax.dot_general(out_grad.astype(jnp.float32), inputs.astype(jnp.float32), (((0,), (0,)), ((), ())), preferred_element_type=jnp.float32)
    grad_half = gradient.astype(jnp.bfloat16)
    right = jnp.dot(grad_half.astype(jnp.float32), a_inverse.astype(jnp.float32), preferred_element_type=jnp.float32).astype(jnp.bfloat16)
    update = jnp.dot(g_inverse.astype(jnp.float32), right.astype(jnp.float32), preferred_element_type=jnp.float32)
    new_momentum = 0.9 * momentum + update
    new_weights = weights - 0.5 * new_momentum
    return new_weights, new_momentum
```

```python
import functools

import jax
import jax.numpy as jnp
from jax import lax
from jax.experimental import pallas as pl
from jax.experimental.pallas import tpu as pltpu
from jax.sharding import PartitionSpec as P

BF = jnp.bfloat16
F32 = jnp.float32
MESH = pl.DeviceIdType.MESH
NZ, NY = 4, 4
IN, OUT, TOK = 4096, 4608, 640
HALF = OUT // 2
RZ = HALF // NZ
SEG = RZ // NY
W = 256
STEPS = IN // (2 * W)
COLS = 128


def coords():
    d = lax.axis_index("dp")
    return d // 16, (d // 4) % 4, (d // 2) % 2, d % 2


def dev(z, y, x, c):
    return {"dp": ((z * 4 + y) * 2 + x) * 2 + c}


def remote(src, dst, ssem, rsem, to):
    return pltpu.make_async_remote_copy(
        src_ref=src, dst_ref=dst, send_sem=ssem, recv_sem=rsem, device_id=to, device_id_type=MESH
    )


def greet(peers):
    barrier = pltpu.get_barrier_semaphore()
    for p in peers:
        pl.semaphore_signal(barrier, inc=1, device_id=p, device_id_type=MESH)
    pl.semaphore_wait(barrier, len(peers))


def reduce_kernel(
    in_ref, og_ref, a_ref, g_ref, xg_out, ag_out, gg_out,
    ogt, ogl, ogr, inb, inr, acc, s1a, s1b, s1c, r1a, r1bc,
    sums, s2a, s2b, s2c, r2a, r2bc, tot, sx, rx, xg,
    load_sem, ld_sem, pair_s, pair_r, s1_sem, r1_sem, s2_sem, r2_sem, x_s, x_r, yg_s, yg_r, fw_s, fw_r, ag_s, ag_r, own_sem,
):
    z, y, x, c = coords()
    core = dev(z, y, x, 1 - c)
    xpeer = dev(z, y, 1 - x, c)
    zs = [dev((z + k) % 4, y, x, c) for k in (1, 2, 3)]
    ys = [dev(z, (y + k) % 4, x, c) for k in (1, 2, 3)]
    greet([core, xpeer] + zs + ys)

    other = pl.multiple_of((1 - c) * HALF, 128)
    mine = pl.multiple_of(c * HALF, 128)

    og_x = remote(og_ref.at[:, pl.ds(other, HALF)], ogr, pair_s.at[0], pair_r.at[0], core)
    og_x.start()

    def in_x(s):
        cols = pl.ds(pl.multiple_of(s * 2 * W, 2 * W), 2 * W)
        return remote(in_ref.at[:, cols], inr.at[:, cols], pair_s.at[1 + s], pair_r.at[1 + s], core)

    for s in range(STEPS):
        in_x(s).start()

    def in_load(s):
        cols = pl.ds(pl.multiple_of(s * 2 * W, 2 * W), 2 * W)
        return pltpu.make_async_copy(in_ref.at[:, cols], inb.at[s % 2], ld_sem.at[s % 2])

    in_load(0).start()

    own_a = pltpu.make_async_copy(a_ref, ag_out.at[z, c], own_sem.at[0])
    own_g = pltpu.make_async_copy(g_ref, gg_out.at[y, x], own_sem.at[1])
    own_a.start()
    own_g.start()
    a_sends = [remote(a_ref, ag_out.at[z, c], ag_s.at[k], ag_r.at[k], zs[k]) for k in range(3)]
    g_sends = [remote(g_ref, gg_out.at[y, x], ag_s.at[3 + k], ag_r.at[3 + k], ys[k]) for k in range(3)]
    a_fwd = remote(ag_out.at[:, c], ag_out.at[:, c], ag_s.at[6], ag_r.at[6], core)
    g_fwd = remote(gg_out.at[:, x], gg_out.at[:, x], ag_s.at[7], ag_r.at[7], xpeer)
    for cp in a_sends + g_sends:
        cp.start()

    part = HALF // 3
    for i in range(3):
        cp = pltpu.make_async_copy(og_ref.at[:, pl.ds(mine + i * part, part)], ogl, load_sem.at[0])
        cp.start()
        cp.wait()

        def turn(j, _, i=i):
            lanes = pl.ds(pl.multiple_of(j * 128, 128), 128)
            ogt[pl.ds(pl.multiple_of(i * part + j * 128, 128), 128), 0:TOK] = ogl[:, lanes].T
            return 0

        lax.fori_loop(0, part // 128, turn, 0)
    og_x.wait()

    def turn_r(j, _):
        lanes = pl.ds(pl.multiple_of(j * 128, 128), 128)
        ogt[pl.ds(pl.multiple_of(j * 128, 128), 128), TOK : 2 * TOK] = ogr[:, lanes].T
        return 0

    lax.fori_loop(0, HALF // 128, turn_r, 0)

    first = (z, y)
    second = (y, z)
    stride1 = (RZ, SEG)
    stride2 = (SEG, RZ)
    axis1 = (zs, ys)
    axis2 = (ys, zs)

    def near(k, d):
        return (k + 1) % 4 if d == 0 else (k + 3) % 4

    def to(axis, d):
        return axis[0] if d == 0 else axis[2]

    def rows(t, k, j):
        return pl.ds(pl.multiple_of(k * stride1[t] + j * stride2[t], 16), SEG)

    def ch(s, t):
        return 2 * s + t

    def send_a(s, t, d):
        p = s % 2
        return remote(s1a.at[t, p, d], r1a.at[ch(s, t), d], s1_sem.at[t, p, 0, d], r1_sem.at[ch(s, t), 0, d], to(axis1[t], d))

    def send_b(s, t, d):
        p = s % 2
        return remote(s1b.at[t, p, d], r1bc.at[ch(s, t), d, 1 - d], s1_sem.at[t, p, 1, d], r1_sem.at[ch(s, t), 1, d], to(axis1[t], d))

    def send_c(s, t, d):
        p = s % 2
        return remote(s1c.at[t, p, d], r1bc.at[ch(s, t), d, d], s1_sem.at[t, p, 2, d], r1_sem.at[ch(s, t), 1, d], to(axis1[t], d))

    def send_2a(s, t, d):
        p = s % 2
        return remote(s2a.at[t, p, d], r2a.at[ch(s, t), d], s2_sem.at[t, p, 0, d], r2_sem.at[ch(s, t), 0, d], to(axis2[t], d))

    def send_2b(s, t, d):
        p = s % 2
        return remote(s2b.at[t, p, d], r2bc.at[ch(s, t), d, 1 - d], s2_sem.at[t, p, 1, d], r2_sem.at[ch(s, t), 1, d], to(axis2[t], d))

    def send_2c(s, t, d):
        p = s % 2
        return remote(s2c.at[t, p, d], r2bc.at[ch(s, t), d, d], s2_sem.at[t, p, 2, d], r2_sem.at[ch(s, t), 1, d], to(axis2[t], d))

    def send_x(s, t):
        p = s % 2
        return remote(sx.at[t, p], rx.at[ch(s, t)], x_s.at[t, p], x_r.at[ch(s, t)], xpeer)

    def tile(s, t):
        return pl.ds(pl.multiple_of(ch(s, t) * W + x * COLS, COLS), COLS)

    def send_y(s, t, k):
        here = xg.at[pl.ds(pl.multiple_of(y * SEG, 16), SEG), tile(s, t)]
        return remote(here, here, yg_s.at[t, s % 2, k], yg_r.at[ch(s, t), k], ys[k])

    def send_fw(s, t):
        here = xg.at[:, tile(s, t)]
        return remote(here, here, fw_s.at[t, s % 2], fw_r.at[ch(s, t)], xpeer)

    def arrived(ref, sem):
        pltpu.make_async_copy(ref, ref, sem).wait()

    def compute(s):
        p = s % 2
        in_load(s).wait()
        in_x(s).wait()

        @pl.when(s + 1 < STEPS)
        def _():
            in_load(s + 1).start()

        for t in range(2):
            b_own = inb[p, :, t * W : (t + 1) * W]
            b_other = inr[:, pl.ds(pl.multiple_of(ch(s, t) * W, W), W)]

            def block(i, _):
                r = pl.ds(pl.multiple_of(i * RZ, 16), RZ)
                v = jnp.dot(ogt[r, 0:TOK], b_own, preferred_element_type=F32)
                v = v + jnp.dot(ogt[r, TOK : 2 * TOK], b_other, preferred_element_type=F32)
                acc[t, p, 0, r, :] = v[:, :COLS]
                acc[t, p, 1, r, :] = v[:, COLS:]
                return 0

            lax.fori_loop(0, NZ, block, 0)
            m = first[t]
            for d in range(2):
                for j in range(4):
                    s1a[t, p, d, j] = acc[t, p, d, rows(t, (m + 2) % 4, j), :].astype(BF)
                send_a(s, t, d).start()
            for d in range(2):
                for j in range(4):
                    s1b[t, p, d, j] = acc[t, p, 1 - d, rows(t, near(m, d), j), :].astype(BF)
                send_b(s, t, d).start()

    def pass_on(s):
        p = s % 2
        for t in range(2):
            for d in range(2):
                arrived(r1a.at[ch(s, t), d], r1_sem.at[ch(s, t), 0, d])
                for j in range(4):
                    v = acc[t, p, d, rows(t, near(first[t], d), j), :] + r1a[ch(s, t), d, j].astype(F32)
                    s1c[t, p, d, j] = v.astype(BF)
                send_c(s, t, d).start()

    def sum_first(s):
        p = s % 2
        for t in range(2):
            for d in range(2):
                arrived(r1bc.at[ch(s, t), d], r1_sem.at[ch(s, t), 1, d])
            for h in range(2):
                for j in range(4):
                    v = acc[t, p, h, rows(t, first[t], j), :]
                    v = v + r1bc[ch(s, t), 0, h, j].astype(F32) + r1bc[ch(s, t), 1, h, j].astype(F32)
                    sums[t, p, h, j] = v
            m = second[t]
            for d in range(2):
                s2a[t, p, d] = sums[t, p, d, (m + 2) % 4].astype(BF)
                send_2a(s, t, d).start()
            for d in range(2):
                s2b[t, p, d] = sums[t, p, 1 - d, near(m, d)].astype(BF)
                send_2b(s, t, d).start()
            for d in range(2):
                send_a(s, t, d).wait_send()
                send_b(s, t, d).wait_send()
                send_c(s, t, d).wait_send()

    def pass_on_second(s):
        p = s % 2
        for t in range(2):
            for d in range(2):
                arrived(r2a.at[ch(s, t), d], r2_sem.at[ch(s, t), 0, d])
                v = sums[t, p, d, near(second[t], d)] + r2a[ch(s, t), d].astype(F32)
                s2c[t, p, d] = v.astype(BF)
                send_2c(s, t, d).start()

    def sum_second(s):
        p = s % 2
        for t in range(2):
            for d in range(2):
                arrived(r2bc.at[ch(s, t), d], r2_sem.at[ch(s, t), 1, d])
            for h in range(2):
                v = sums[t, p, h, second[t]]
                tot[t, p, h] = v + r2bc[ch(s, t), 0, h].astype(F32) + r2bc[ch(s, t), 1, h].astype(F32)
            sx[t, p] = tot[t, p, 1 - x]
            send_x(s, t).start()
            for d in range(2):
                send_2a(s, t, d).wait_send()
                send_2b(s, t, d).wait_send()
                send_2c(s, t, d).wait_send()

    def finish(s):
        p = s % 2
        for t in range(2):
            send_x(s, t).wait()
            v = tot[t, p, x] + rx[ch(s, t)]
            xg[pl.ds(pl.multiple_of(y * SEG, 16), SEG), tile(s, t)] = v.astype(BF)
            for k in range(3):
                send_y(s, t, k).start()

    def forward(s):
        for t in range(2):
            for k in range(3):
                send_y(s, t, k).wait()
            send_fw(s, t).start()

    def complete(s):
        for t in range(2):
            send_fw(s, t).wait()

    stages = [(7, complete), (6, forward), (5, finish), (4, sum_second), (3, pass_on_second), (2, sum_first), (1, pass_on), (0, compute)]

    def step(s, _):
        for lag, stage in stages:

            @pl.when(jnp.logical_and(s >= lag, s < STEPS + lag))
            def _(lag=lag, stage=stage):
                stage(s - lag)

        @pl.when(s == 2)
        def _():
            own_a.wait()
            for cp in a_sends:
                cp.wait()
            a_fwd.start()

        @pl.when(s == 3)
        def _():
            own_g.wait()
            for cp in g_sends:
                cp.wait()
            g_fwd.start()

        return 0

    lax.fori_loop(0, STEPS + 7, step, 0)
    out = pltpu.make_async_copy(xg, xg_out, load_sem.at[0])
    out.start()
    a_fwd.wait()
    g_fwd.wait()
    out.wait()


def reduce_call(inputs, out_grad, a_inverse, g_inverse):
    anyspace = pl.BlockSpec(memory_space=pl.ANY)
    n = 2 * STEPS
    dma = pltpu.SemaphoreType.DMA
    return pl.pallas_call(
        reduce_kernel,
        out_shape=[
            jax.ShapeDtypeStruct((RZ, IN), BF),
            jax.ShapeDtypeStruct((4, 2, IN // 64, IN), BF),
            jax.ShapeDtypeStruct((4, 2, OUT // 64, OUT), BF),
        ],
        in_specs=[anyspace] * 4,
        out_specs=[anyspace] * 3,
        scratch_shapes=[
            pltpu.VMEM((HALF, 2 * TOK), BF),
            pltpu.VMEM((TOK, HALF // 3), BF),
            pltpu.VMEM((TOK, HALF), BF),
            pltpu.VMEM((2, TOK, 2 * W), BF),
            pltpu.VMEM((TOK, IN), BF),
            pltpu.VMEM((2, 2, 2, HALF, COLS), F32),
            pltpu.VMEM((2, 2, 2, 4, SEG, COLS), BF),
            pltpu.VMEM((2, 2, 2, 4, SEG, COLS), BF),
            pltpu.VMEM((2, 2, 2, 4, SEG, COLS), BF),
            pltpu.VMEM((n, 2, 4, SEG, COLS), BF),
            pltpu.VMEM((n, 2, 2, 4, SEG, COLS), BF),
            pltpu.VMEM((2, 2, 2, 4, SEG, COLS), F32),
            pltpu.VMEM((2, 2, 2, SEG, COLS), BF),
            pltpu.VMEM((2, 2, 2, SEG, COLS), BF),
            pltpu.VMEM((2, 2, 2, SEG, COLS), BF),
            pltpu.VMEM((n, 2, SEG, COLS), BF),
            pltpu.VMEM((n, 2, 2, SEG, COLS), BF),
            pltpu.VMEM((2, 2, 2, SEG, COLS), F32),
            pltpu.VMEM((2, 2, SEG, COLS), F32),
            pltpu.VMEM((n, SEG, COLS), F32),
            pltpu.VMEM((RZ, IN), BF),
            dma((1,)),
            dma((2,)),
            dma((1 + STEPS,)),
            dma((1 + STEPS,)),
            dma((2, 2, 3, 2)),
            dma((n, 2, 2)),
            dma((2, 2, 3, 2)),
            dma((n, 2, 2)),
            dma((2, 2)),
            dma((n,)),
            dma((2, 2, 3)),
            dma((n, 3)),
            dma((2, 2)),
            dma((n,)),
            dma((8,)),
            dma((8,)),
            dma((2,)),
        ],
        compiler_params=pltpu.CompilerParams(
            collective_id=0, has_side_effects=True, vmem_limit_bytes=62 * 1024 * 1024
        ),
        cost_estimate=pl.CostEstimate(flops=24_200_000_000, bytes_accessed=40_000_000, transcendentals=0),
        name="gradient_reduce",
    )(inputs, out_grad, a_inverse, g_inverse)


def update_kernel(xg, ag, gg, u_out, rg, ub, uo, z_s, z_r, c_s, c_r, u_s, u_r, out_sem):
    z, y, x, c = coords()
    core = dev(z, y, x, 1 - c)
    zs = [dev((z + k) % 4, y, x, c) for k in (1, 2, 3)]
    offs = [(k, e) for k in range(4) for e in range(2) if (k, e) != (0, 0)]
    yx = [dev(z, (y + k) % 4, (x + e) % 2, c) for k, e in offs]
    greet([core] + zs + yx)
    my_rows = pl.ds(pl.multiple_of(c * HALF + z * RZ, 16), RZ)
    core_rows = pl.ds(pl.multiple_of(c * HALF, 16), HALF)

    def send_z(q, k):
        here = rg.at[q, my_rows]
        return remote(here, here, z_s.at[q, k], z_r.at[q, k], zs[k])

    def send_core(q):
        here = rg.at[q, core_rows]
        return remote(here, here, c_s.at[q], c_r.at[q], core)

    def tile(q):
        return pl.ds(pl.multiple_of(((q * 4 + y) * 2 + x) * COLS, COLS), COLS)

    def send_u(q, i):
        k, e = offs[i]
        owner = ((y + k) % 4) * 2 + (x + e) % 2
        return remote(ub.at[q, owner], uo.at[:, tile(q)], u_s.at[q, i], u_r.at[q, i], yx[i])

    def right(q, _):
        a_rows = ag[pl.ds(pl.multiple_of(q * COLS, COLS), COLS), :]
        v = lax.dot_general(xg[...], a_rows, (((1,), (1,)), ((), ())), preferred_element_type=F32)
        rg[q, my_rows, :] = v.astype(BF)
        for k in range(3):
            send_z(q, k).start()
        return 0

    def update(q):
        send_core(q).wait()
        v = jnp.dot(gg[...], rg[q], preferred_element_type=F32)
        ub[q] = v.reshape(8, OUT // 64, COLS)
        uo[:, tile(q)] = ub[q, y * 2 + x]
        for i in range(7):
            send_u(q, i).start()

    def gather(q, _):
        @pl.when(q < 4)
        def _():
            for k in range(3):
                send_z(q, k).wait()
            send_core(q).start()

        @pl.when(q > 0)
        def _():
            update(q - 1)

        return 0

    lax.fori_loop(0, 4, right, 0)
    lax.fori_loop(0, 5, gather, 0)

    def done(q, _):
        for i in range(7):
            send_u(q, i).wait()
        return 0

    lax.fori_loop(0, 4, done, 0)
    cp = pltpu.make_async_copy(uo, u_out, out_sem.at[0])
    cp.start()
    cp.wait()


def update_call(xg, ag, gg):
    dma = pltpu.SemaphoreType.DMA
    vmem = pl.BlockSpec(memory_space=pltpu.VMEM)
    return pl.pallas_call(
        update_kernel,
        out_shape=jax.ShapeDtypeStruct((OUT // 64, IN), F32),
        in_specs=[vmem] * 3,
        out_specs=pl.BlockSpec(memory_space=pl.ANY),
        scratch_shapes=[
            pltpu.VMEM((4, OUT, COLS), BF),
            pltpu.VMEM((4, 8, OUT // 64, COLS), F32),
            pltpu.VMEM((OUT // 64, IN), F32),
            dma((4, 3)),
            dma((4, 3)),
            dma((4,)),
            dma((4,)),
            dma((4, 7)),
            dma((4, 7)),
            dma((1,)),
        ],
        compiler_params=pltpu.CompilerParams(
            collective_id=1, has_side_effects=True, vmem_limit_bytes=56 * 1024 * 1024
        ),
        cost_estimate=pl.CostEstimate(flops=5_200_000_000, bytes_accessed=16_000_000, transcendentals=0),
        name="precondition",
    )(xg, ag, gg)


def per_device(inputs, out_grad, a_inverse, g_inverse, weights, momentum):
    xg, ag, gg = reduce_call(inputs, out_grad, a_inverse, g_inverse)
    update = update_call(xg, ag.reshape(IN // 8, IN), gg.reshape(OUT // 8, OUT))
    new_momentum = 0.9 * momentum + update
    new_weights = weights - 0.5 * new_momentum
    return (new_weights, new_momentum)


def solution(mesh):
    spec = P(("pipe", "dp"), None)
    return jax.shard_map(
        per_device, mesh=mesh, in_specs=(spec,) * 6, out_specs=(spec, spec), check_vma=False
    )
```

```python
import functools

import jax
import jax.numpy as jnp
from jax import lax
from jax.experimental import pallas as pl
from jax.experimental.pallas import tpu as pltpu
from jax.sharding import PartitionSpec as P

BF = jnp.bfloat16
F32 = jnp.float32
MESH = pl.DeviceIdType.MESH
NZ, NY = 4, 4
IN, OUT, TOK = 4096, 4608, 640
HALF = OUT // 2
RZ = HALF // NZ
SEG = RZ // NY
W = 256
STEPS = IN // (2 * W)
COLS = 128
LAST = STEPS + 6
G_PAIR = 11
GK = OUT // 4
SLICE = 512
A_SLICES = IN // SLICE


def coords():
    d = lax.axis_index("dp")
    return d // 16, (d // 4) % 4, (d // 2) % 2, d % 2


def dev(z, y, x, c):
    return {"dp": ((z * 4 + y) * 2 + x) * 2 + c}


def remote(src, dst, ssem, rsem, to):
    return pltpu.make_async_remote_copy(
        src_ref=src, dst_ref=dst, send_sem=ssem, recv_sem=rsem, device_id=to, device_id_type=MESH
    )


def greet(peers):
    barrier = pltpu.get_barrier_semaphore()
    for p in peers:
        pl.semaphore_signal(barrier, inc=1, device_id=p, device_id_type=MESH)
    pl.semaphore_wait(barrier, len(peers))


def reduce_kernel(
    in_ref, og_ref, a_ref, g_ref, u_out, ag_hbm, gg_hbm,
    ogt, ogr, inb, inr, acc, s1a, s1b, s1c, r1a, r1bc,
    sums, s2a, s2b, s2c, r2a, r2bc, tot, sx, rx, xg,
    load_sem, ld_sem, pair_s, pair_r, s1_sem, r1_sem, s2_sem, r2_sem, x_s, x_r, yg_s, yg_r, fw_s, fw_r, ag_s, ag_r, ra_s, ra_r, gp_s, gp_r, gf_s, gf_r, own_sem,
    al_sem, gl_sem, gst, rg, uo, z_s, z_r, c_s, c_r, u_s, u_r,
):
    z, y, x, c = coords()
    core = dev(z, y, x, 1 - c)
    xpeer = dev(z, y, 1 - x, c)
    zs = [dev((z + k) % 4, y, x, c) for k in (1, 2, 3)]
    ys = [dev(z, (y + k) % 4, x, c) for k in (1, 2, 3)]
    offs = [(k, e) for k in range(4) for e in range(2) if (k, e) != (0, 0)]
    yx = [dev(z, (y + k) % 4, (x + e) % 2, c) for k, e in offs]
    greet([core, zs[0], zs[2]] + yx)
    my_rows = pl.ds(pl.multiple_of(c * HALF + z * RZ, 16), RZ)
    core_rows = pl.ds(pl.multiple_of(c * HALF, 16), HALF)

    other = pl.multiple_of((1 - c) * HALF, 128)
    mine = pl.multiple_of(c * HALF, 128)

    og_x = remote(og_ref.at[:, pl.ds(other, HALF)], ogr, pair_s.at[0], pair_r.at[0], core)
    og_x.start()

    def in_x(s):
        cols = pl.ds(pl.multiple_of(s * 2 * W, 2 * W), 2 * W)
        return remote(in_ref.at[:, cols], inr.at[:, cols], pair_s.at[1 + s], pair_r.at[1 + s], core)

    for s in range(STEPS):
        in_x(s).start()

    def in_load(s):
        cols = pl.ds(pl.multiple_of(s * 2 * W, 2 * W), 2 * W)
        return pltpu.make_async_copy(in_ref.at[:, cols], inb.at[s % 2], ld_sem.at[s % 2])


    own_a = pltpu.make_async_copy(a_ref, ag_hbm.at[z, c], own_sem.at[0])
    own_g = pltpu.make_async_copy(g_ref, gg_hbm.at[y, x], own_sem.at[1])
    own_a.start()
    own_g.start()
    a_sends = [remote(a_ref, ag_hbm.at[z, c], ag_s.at[k], ag_r.at[k], zs[2 * k]) for k in range(2)]
    g_sends = [remote(g_ref, gg_hbm.at[y, x], ag_s.at[2 + k], ag_r.at[2 + k], ys[2 * k]) for k in range(2)]
    a_fwd = remote(ag_hbm.at[:, c], ag_hbm.at[:, c], ag_s.at[4], ag_r.at[4], core)
    g_own = remote(g_ref, gg_hbm.at[y, x], ag_s.at[5], ag_r.at[5], xpeer)
    for cp in a_sends + g_sends + [g_own]:
        cp.start()

    def relay(out, sem, i, k, other_k, axis, d):
        cols = pl.ds(pl.multiple_of(i * SLICE, SLICE), SLICE)
        from_k = (k + 3) % 4 if d == 0 else (k + 1) % 4
        here = out.at[from_k, other_k, :, cols]
        return remote(here, here, sem[0].at[i], sem[1].at[i], axis[2 * d])

    def relay_a(i, d):
        return relay(ag_hbm, (ra_s, ra_r), i, z, c, zs, d)

    def g_pair(d):
        here = gg_hbm.at[y, 1 - x]
        return remote(here, here, gp_s.at[d], gp_r.at[d], ys[2 * d])

    def g_far(e, d):
        half = OUT // 2
        here = gg_hbm.at[(y + 3 - 2 * d) % 4, e, :, d * half : (d + 1) * half]
        return remote(here, here, gf_s.at[e, d], gf_r.at[e, d], ys[2 * d])

    a_loads = [
        pltpu.make_async_copy(ag_hbm.at[i // 2, i % 2], inr.at[i * 64 : (i + 1) * 64], al_sem.at[i]) for i in range(8)
    ]

    def g_load(b):
        cols = pl.ds(b * GK, GK)
        return pltpu.make_async_copy(gg_hbm.at[:, :, :, cols], gst.at[b % 2], gl_sem.at[b % 2])

    def between(s, lo, n):
        return jnp.logical_and(s >= lo, s < lo + n)

    def background(s):
        @pl.when(s == 1)
        def _():
            for cp in a_sends:
                cp.wait()

        @pl.when(s == G_PAIR)
        def _():
            g_own.wait()
            for d in range(2):
                g_pair(d).start()

        @pl.when(between(s, 1, A_SLICES // 2))
        def _():
            relay_a(2 * (s - 1), 0).start()
            relay_a(2 * (s - 1) + 1, 1).start()

        @pl.when(between(s, 3, A_SLICES // 2))
        def _():
            relay_a(2 * (s - 3), 0).wait()
            relay_a(2 * (s - 3) + 1, 1).wait()

        @pl.when(s == 3 + A_SLICES // 2)
        def _():
            own_a.wait()
            a_fwd.start()

        @pl.when(s == 5 + A_SLICES // 2)
        def _():
            a_fwd.wait()
            for cp in a_loads:
                cp.start()

    part = HALF // 6

    def og_load(i):
        return pltpu.make_async_copy(
            og_ref.at[:, pl.ds(mine + i * part, part)], inb.at[i % 2, :, 0:part], ld_sem.at[i % 2]
        )

    og_load(0).start()
    for i in range(6):
        if i < 5:
            og_load(i + 1).start()
        og_load(i).wait()
        for j in range(part // 128):
            ogt[i * part + j * 128 : i * part + (j + 1) * 128, 0:TOK] = inb[i % 2, :, j * 128 : (j + 1) * 128].T
    in_load(0).start()
    og_x.wait()

    def turn_r(j, _):
        lanes = pl.ds(pl.multiple_of(j * 128, 128), 128)
        ogt[pl.ds(pl.multiple_of(j * 128, 128), 128), TOK : 2 * TOK] = ogr[:, lanes].T
        return 0

    lax.fori_loop(0, HALF // 128, turn_r, 0)

    def kind(s, t):
        return t

    def first(s, t):
        return z + kind(s, t) * (y - z)

    def second(s, t):
        return y + kind(s, t) * (z - y)

    def to(s, t, stage, d):
        e = kind(s, t) if stage == 1 else 1 - kind(s, t)
        k = 1 if d == 0 else 3
        return dev((z + (1 - e) * k) % 4, (y + e * k) % 4, x, c)

    def near(k, d):
        return (k + 1) % 4 if d == 0 else (k + 3) % 4

    def rows(s, t, k, j):
        stride1 = RZ + kind(s, t) * (SEG - RZ)
        return pl.ds(pl.multiple_of(k * stride1 + j * (RZ + SEG - stride1), 16), SEG)

    def ch(s, t):
        return 2 * s + t

    def send_a(s, t, d):
        p = s % 2
        return remote(s1a.at[t, p, d], r1a.at[ch(s, t), d], s1_sem.at[t, p, 0, d], r1_sem.at[ch(s, t), 0, d], to(s, t, 1, d))

    def send_b(s, t, d):
        p = s % 2
        return remote(s1b.at[t, p, d], r1bc.at[ch(s, t), d, 1 - d], s1_sem.at[t, p, 1, d], r1_sem.at[ch(s, t), 1, d], to(s, t, 1, d))

    def send_c(s, t, d):
        p = s % 2
        return remote(s1c.at[t, p, d], r1bc.at[ch(s, t), d, d], s1_sem.at[t, p, 2, d], r1_sem.at[ch(s, t), 1, d], to(s, t, 1, d))

    def send_2a(s, t, d):
        p = s % 2
        return remote(s2a.at[t, p, d], r2a.at[ch(s, t), d], s2_sem.at[t, p, 0, d], r2_sem.at[ch(s, t), 0, d], to(s, t, 2, d))

    def send_2b(s, t, d):
        p = s % 2
        return remote(s2b.at[t, p, d], r2bc.at[ch(s, t), d, 1 - d], s2_sem.at[t, p, 1, d], r2_sem.at[ch(s, t), 1, d], to(s, t, 2, d))

    def send_2c(s, t, d):
        p = s % 2
        return remote(s2c.at[t, p, d], r2bc.at[ch(s, t), d, d], s2_sem.at[t, p, 2, d], r2_sem.at[ch(s, t), 1, d], to(s, t, 2, d))

    def send_x(s, t):
        p = s % 2
        return remote(sx.at[t, p], rx.at[ch(s, t)], x_s.at[t, p], x_r.at[ch(s, t)], xpeer)

    def tile(s, t):
        return pl.ds(pl.multiple_of(ch(s, t) * W + x * COLS, COLS), COLS)

    def send_y(s, t, d):
        here = xg.at[pl.ds(pl.multiple_of(y * SEG, 16), SEG), tile(s, t)]
        return remote(here, here, yg_s.at[t, s % 2, d], yg_r.at[ch(s, t), d], ys[2 * d])

    def relay_y(s, t):
        behind = near(y, 1 - t)
        here = xg.at[pl.ds(pl.multiple_of(behind * SEG, 16), SEG), tile(s, t)]
        return remote(here, here, yg_s.at[t, s % 2, 2], yg_r.at[ch(s, t), 2], ys[2 * t])

    def send_fw(s, t, k):
        here = xg.at[pl.ds(pl.multiple_of(((y + k) % 4) * SEG, 16), SEG), tile(s, t)]
        return remote(here, here, fw_s.at[ch(s, t), k], fw_r.at[ch(s, t), k], xpeer)

    def arrived(ref, sem):
        pltpu.make_async_copy(ref, ref, sem).wait()

    def fetch(s):
        in_load(s).wait()
        in_x(s).wait()

        @pl.when(s + 1 < STEPS)
        def _():
            in_load(s + 1).start()

    def compute(s, ts):
        p = s % 2
        for t in ts:
            b_own = inb[p, :, t * W : (t + 1) * W]
            b_other = inr[:, pl.ds(pl.multiple_of(ch(s, t) * W, W), W)]

            def block(i, _):
                r = pl.ds(pl.multiple_of(i * RZ, 16), RZ)
                v = jnp.dot(ogt[r, 0:TOK], b_own, preferred_element_type=F32)
                v = v + jnp.dot(ogt[r, TOK : 2 * TOK], b_other, preferred_element_type=F32)
                acc[t, p, 0, r, :] = v[:, :COLS]
                acc[t, p, 1, r, :] = v[:, COLS:]
                return 0

            lax.fori_loop(0, NZ, block, 0)

    def send_first(s, ts):
        p = s % 2
        for t in ts:
            m = first(s, t)
            for d in range(2):
                for j in range(4):
                    s1a[t, p, d, j] = acc[t, p, d, rows(s, t, (m + 2) % 4, j), :].astype(BF)
                send_a(s, t, d).start()
            for d in range(2):
                for j in range(4):
                    s1b[t, p, d, j] = acc[t, p, 1 - d, rows(s, t, near(m, d), j), :].astype(BF)
                send_b(s, t, d).start()

    def pass_on(s):
        p = s % 2
        for t in range(2):
            for d in range(2):
                arrived(r1a.at[ch(s, t), d], r1_sem.at[ch(s, t), 0, d])
                for j in range(4):
                    v = acc[t, p, d, rows(s, t, near(first(s, t), d), j), :] + r1a[ch(s, t), d, j].astype(F32)
                    s1c[t, p, d, j] = v.astype(BF)
                send_c(s, t, d).start()

    def sum_first(s):
        p = s % 2
        for t in range(2):
            for d in range(2):
                arrived(r1bc.at[ch(s, t), d], r1_sem.at[ch(s, t), 1, d])
            for h in range(2):
                for j in range(4):
                    v = acc[t, p, h, rows(s, t, first(s, t), j), :]
                    v = v + r1bc[ch(s, t), 0, h, j].astype(F32) + r1bc[ch(s, t), 1, h, j].astype(F32)
                    sums[t, p, h, j] = v
            m = second(s, t)
            for d in range(2):
                s2a[t, p, d] = sums[t, p, d, (m + 2) % 4].astype(BF)
                send_2a(s, t, d).start()
            for d in range(2):
                s2b[t, p, d] = sums[t, p, 1 - d, near(m, d)].astype(BF)
                send_2b(s, t, d).start()
            for d in range(2):
                send_a(s, t, d).wait_send()
                send_b(s, t, d).wait_send()
                send_c(s, t, d).wait_send()

    def pass_on_second(s):
        p = s % 2
        for t in range(2):
            for d in range(2):
                arrived(r2a.at[ch(s, t), d], r2_sem.at[ch(s, t), 0, d])
                v = sums[t, p, d, near(second(s, t), d)] + r2a[ch(s, t), d].astype(F32)
                s2c[t, p, d] = v.astype(BF)
                send_2c(s, t, d).start()

    def sum_second(s):
        p = s % 2
        for t in range(2):
            for d in range(2):
                arrived(r2bc.at[ch(s, t), d], r2_sem.at[ch(s, t), 1, d])
            for h in range(2):
                v = sums[t, p, h, second(s, t)]
                tot[t, p, h] = v + r2bc[ch(s, t), 0, h].astype(F32) + r2bc[ch(s, t), 1, h].astype(F32)
            sx[t, p] = tot[t, p, 1 - x]
            send_x(s, t).start()
            for d in range(2):
                send_2a(s, t, d).wait_send()
                send_2b(s, t, d).wait_send()
                send_2c(s, t, d).wait_send()

    def finish(s):
        p = s % 2
        for t in range(2):
            send_x(s, t).wait()
            v = tot[t, p, x] + rx[ch(s, t)]
            xg[pl.ds(pl.multiple_of(y * SEG, 16), SEG), tile(s, t)] = v.astype(BF)
            for d in range(2):
                send_y(s, t, d).start()
            send_fw(s, t, 0).start()

    def relay_tiles(s):
        for t in range(2):
            for d in range(2):
                send_y(s, t, d).wait()
            relay_y(s, t).start()
            send_fw(s, t, 1).start()
            send_fw(s, t, 3).start()

    def forward(s):
        for t in range(2):
            relay_y(s, t).wait()
            send_fw(s, t, 2).start()

    def complete(s):
        for t in range(2):
            for k in range(4):
                send_fw(s, t, k).wait()

    stages = [
        (2, sum_first),
        (1, pass_on),
        (3, sum_second),
        (4, relay_tiles),
        (0, fetch),
        (0, lambda s: compute(s, (0,))),
        (2, pass_on_second),
        (0, lambda s: send_first(s, (0,))),
        (0, lambda s: compute(s, (1,))),
        (0, lambda s: send_first(s, (1,))),
        (3, finish),
        (6, complete),
        (4, forward),
    ]

    def step(s, _):
        for lag, stage in stages:

            @pl.when(jnp.logical_and(s >= lag, s < STEPS + lag))
            def _(lag=lag, stage=stage):
                stage(s - lag)

        background(s)
        return 0

    lax.fori_loop(0, LAST, step, 0)
    for cp in a_loads:
        cp.wait()

    def send_r(q, d):
        here = rg.at[q, my_rows]
        return remote(here, here, z_s.at[q, d], z_r.at[q, d], zs[2 * d])

    def relay_r(q):
        d = q % 2
        behind = near(z, 1 - d)
        here = rg.at[q, pl.ds(pl.multiple_of(c * HALF + behind * RZ, 16), RZ)]
        return remote(here, here, z_s.at[q, 2], z_r.at[q, 2], zs[2 * d])

    def send_core(q):
        here = rg.at[q, core_rows]
        return remote(here, here, c_s.at[q], c_r.at[q], core)

    def utile(q):
        return pl.ds(pl.multiple_of(((q * 4 + y) * 2 + x) * COLS, COLS), COLS)

    def urows(owner):
        return pl.ds(pl.multiple_of(owner * (OUT // 64), 8), OUT // 64)

    def send_u(q, i):
        k, e = offs[i]
        owner = ((y + k) % 4) * 2 + (x + e) % 2
        return remote(acc.at[q // 2, q % 2, 0, urows(owner)], uo.at[:, utile(q)], u_s.at[q, i], u_r.at[q, i], yx[i])

    for q in range(4):
        v = lax.dot_general(
            xg[...], inr[q * COLS : (q + 1) * COLS, :], (((1,), (1,)), ((), ())), preferred_element_type=F32
        )
        rg[q, my_rows, :] = v.astype(BF)
        for d in range(2):
            send_r(q, d).start()
    own_g.wait()
    for cp in g_sends:
        cp.wait()
    for d in range(2):
        g_pair(d).wait()
    for e in range(2):
        for d in range(2):
            g_far(e, d).start()

    for q in range(5):
        if q < 4:
            for d in range(2):
                send_r(q, d).wait()
            relay_r(q).start()
        if q >= 1:
            relay_r(q - 1).wait()
            send_core(q - 1).start()
    for e in range(2):
        for d in range(2):
            g_far(e, d).wait()
    g_load(0).start()
    for b in range(4):
        if b < 3:
            g_load(b + 1).start()
        g_load(b).wait()
        for i in range(4):
            v = jnp.concatenate([gst[b % 2, i, 0], gst[b % 2, i, 1]], axis=0)
            ogt[b * RZ + i * SEG : b * RZ + (i + 1) * SEG, 0:GK] = v
    for w in range(4):
        send_core(w).wait()
        v = jnp.zeros((RZ, COLS), F32)
        for b in range(4):
            v = v + jnp.dot(
                ogt[b * RZ : (b + 1) * RZ, 0:GK], rg[w, b * GK : (b + 1) * GK, :], preferred_element_type=F32
            )
        acc[w // 2, w % 2, 0, 0:RZ, :] = v
        uo[:, utile(w)] = acc[w // 2, w % 2, 0, urows(y * 2 + x), :]
        for i in range(7):
            send_u(w, i).start()
    for q in range(4):
        for i in range(7):
            send_u(q, i).wait()
    cp = pltpu.make_async_copy(uo, u_out, load_sem.at[0])
    cp.start()
    cp.wait()


def reduce_call(inputs, out_grad, a_inverse, g_inverse):
    anyspace = pl.BlockSpec(memory_space=pl.ANY)
    n = 2 * STEPS
    dma = pltpu.SemaphoreType.DMA
    return pl.pallas_call(
        reduce_kernel,
        out_shape=[
            jax.ShapeDtypeStruct((OUT // 64, IN), F32),
            jax.ShapeDtypeStruct((4, 2, IN // 64, IN), BF),
            jax.ShapeDtypeStruct((4, 2, OUT // 64, OUT), BF),
        ],
        in_specs=[anyspace] * 4,
        out_specs=[anyspace] * 3,
        scratch_shapes=[
            pltpu.VMEM((HALF, 2 * TOK), BF),
            pltpu.VMEM((TOK, HALF), BF),
            pltpu.VMEM((2, TOK, 2 * W), BF),
            pltpu.VMEM((TOK, IN), BF),
            pltpu.VMEM((2, 2, 2, HALF, COLS), F32),
            pltpu.VMEM((2, 2, 2, 4, SEG, COLS), BF),
            pltpu.VMEM((2, 2, 2, 4, SEG, COLS), BF),
            pltpu.VMEM((2, 2, 2, 4, SEG, COLS), BF),
            pltpu.VMEM((n, 2, 4, SEG, COLS), BF),
            pltpu.VMEM((n, 2, 2, 4, SEG, COLS), BF),
            pltpu.VMEM((2, 2, 2, 4, SEG, COLS), F32),
            pltpu.VMEM((2, 2, 2, SEG, COLS), BF),
            pltpu.VMEM((2, 2, 2, SEG, COLS), BF),
            pltpu.VMEM((2, 2, 2, SEG, COLS), BF),
            pltpu.VMEM((n, 2, SEG, COLS), BF),
            pltpu.VMEM((n, 2, 2, SEG, COLS), BF),
            pltpu.VMEM((2, 2, 2, SEG, COLS), F32),
            pltpu.VMEM((2, 2, SEG, COLS), F32),
            pltpu.VMEM((n, SEG, COLS), F32),
            pltpu.VMEM((RZ, IN), BF),
            dma((1,)),
            dma((2,)),
            dma((1 + STEPS,)),
            dma((1 + STEPS,)),
            dma((2, 2, 3, 2)),
            dma((n, 2, 2)),
            dma((2, 2, 3, 2)),
            dma((n, 2, 2)),
            dma((2, 2)),
            dma((n,)),
            dma((2, 2, 3)),
            dma((n, 3)),
            dma((n, 4)),
            dma((n, 4)),
            dma((6,)),
            dma((6,)),
            dma((A_SLICES,)),
            dma((A_SLICES,)),
            dma((2,)),
            dma((2,)),
            dma((2, 2)),
            dma((2, 2)),
            dma((2,)),
            dma((8,)),
            dma((2,)),
            pltpu.VMEM((2, 4, 2, OUT // 64, GK), BF),
            pltpu.VMEM((4, OUT, COLS), BF),
            pltpu.VMEM((OUT // 64, IN), F32),
            dma((4, 3)),
            dma((4, 3)),
            dma((4,)),
            dma((4,)),
            dma((4, 7)),
            dma((4, 7)),
        ],
        compiler_params=pltpu.CompilerParams(
            collective_id=0, has_side_effects=True, vmem_limit_bytes=63 * 1024 * 1024
        ),
        cost_estimate=pl.CostEstimate(flops=29_400_000_000, bytes_accessed=40_000_000, transcendentals=0),
        name="kfac_update",
    )(inputs, out_grad, a_inverse, g_inverse)


def per_device(inputs, out_grad, a_inverse, g_inverse, weights, momentum):
    update = reduce_call(inputs, out_grad, a_inverse, g_inverse)[0]
    new_momentum = 0.9 * momentum + update
    new_weights = weights - 0.5 * new_momentum
    return (new_weights, new_momentum)


def solution(mesh):
    spec = P(("pipe", "dp"), None)
    return jax.shard_map(
        per_device, mesh=mesh, in_specs=(spec,) * 6, out_specs=(spec, spec), check_vma=False
    )
```

```python
import functools

import jax
import jax.numpy as jnp
from jax import lax
from jax.experimental import pallas as pl
from jax.experimental.pallas import tpu as pltpu
from jax.sharding import PartitionSpec as P

BF = jnp.bfloat16
F32 = jnp.float32
MESH = pl.DeviceIdType.MESH
NZ, NY = 4, 4
IN, OUT, TOK = 4096, 4608, 640
HALF = OUT // 2
RZ = HALF // NZ
SEG = RZ // NY
W = 256
STEPS = IN // (2 * W)
COLS = 128
ROWHALF = (slice(0, 80), slice(80, 144))
LAST = STEPS + 6
G_PAIR, G_PACK = 11, 13
GK = OUT // 4
SLICE = 512
A_SLICES = IN // SLICE


def coords():
    d = lax.axis_index("dp")
    return d // 16, (d // 4) % 4, (d // 2) % 2, d % 2


def dev(z, y, x, c):
    return {"dp": ((z * 4 + y) * 2 + x) * 2 + c}


def remote(src, dst, ssem, rsem, to):
    return pltpu.make_async_remote_copy(
        src_ref=src, dst_ref=dst, send_sem=ssem, recv_sem=rsem, device_id=to, device_id_type=MESH
    )


def greet(peers):
    barrier = pltpu.get_barrier_semaphore()
    for p in peers:
        pl.semaphore_signal(barrier, inc=1, device_id=p, device_id_type=MESH)
    pl.semaphore_wait(barrier, len(peers))


def reduce_kernel(
    in_ref, og_ref, a_ref, g_ref, u_out, ag_hbm, gg_hbm,
    ogt, ogr, inb, inr, acc, s1, r1a, r1bc,
    sums0, mx, qx, m2, q2a, q2bc, sums, s2, r2a, r2bc, tot, sx, rx, xg,
    load_sem, ld_sem, pair_s, pair_r, s1_sem, r1_sem, s2_sem, r2_sem, x_s, x_r, yg_s, yg_r, fw_s, fw_r, ag_s, ag_r, ra_s, ra_r, gp_s, gp_r, gf_s, gf_r, own_sem,
    al_sem, gl_sem, gst, rg, uo, z_s, z_r, c_s, c_r, u_s, u_r,
):
    z, y, x, c = coords()
    core = dev(z, y, x, 1 - c)
    xpeer = dev(z, y, 1 - x, c)
    zs = [dev((z + k) % 4, y, x, c) for k in (1, 2, 3)]
    ys = [dev(z, (y + k) % 4, x, c) for k in (1, 2, 3)]
    offs = [(k, e) for k in range(4) for e in range(2) if (k, e) != (0, 0)]
    yx = [dev(z, (y + k) % 4, (x + e) % 2, c) for k, e in offs]
    greet([core] + zs + yx)
    my_rows = pl.ds(pl.multiple_of(c * HALF + z * RZ, 16), RZ)
    core_rows = pl.ds(pl.multiple_of(c * HALF, 16), HALF)

    other = pl.multiple_of((1 - c) * HALF, 128)
    mine = pl.multiple_of(c * HALF, 128)

    og_x = remote(og_ref.at[:, pl.ds(other, HALF)], ogr, pair_s.at[0], pair_r.at[0], core)
    og_x.start()

    def in_x(s):
        cols = pl.ds(pl.multiple_of(s * 2 * W, 2 * W), 2 * W)
        return remote(in_ref.at[:, cols], inr.at[:, cols], pair_s.at[1 + s], pair_r.at[1 + s], core)

    in_x(0).start()

    def in_load(s):
        cols = pl.ds(pl.multiple_of(s * 2 * W, 2 * W), 2 * W)
        return pltpu.make_async_copy(in_ref.at[:, cols], inb.at[s % 2], ld_sem.at[s % 2])


    own_a = pltpu.make_async_copy(a_ref, ag_hbm.at[z, c], own_sem.at[0])
    own_g = pltpu.make_async_copy(g_ref, gg_hbm.at[y, x], own_sem.at[1])
    own_a.start()
    own_g.start()
    a_sends = [remote(a_ref, ag_hbm.at[z, c], ag_s.at[k], ag_r.at[k], zs[2 * k]) for k in range(2)]
    g_sends = [remote(g_ref, gg_hbm.at[y, x], ag_s.at[2 + k], ag_r.at[2 + k], ys[2 * k]) for k in range(2)]
    a_fwd = remote(ag_hbm.at[:, c], ag_hbm.at[:, c], ag_s.at[4], ag_r.at[4], core)
    g_own = remote(g_ref, gg_hbm.at[y, x], ag_s.at[5], ag_r.at[5], xpeer)
    for cp in a_sends + g_sends + [g_own]:
        cp.start()

    def relay(out, sem, i, k, other_k, axis, d):
        cols = pl.ds(pl.multiple_of(i * SLICE, SLICE), SLICE)
        from_k = (k + 3) % 4 if d == 0 else (k + 1) % 4
        here = out.at[from_k, other_k, :, cols]
        return remote(here, here, sem[0].at[i], sem[1].at[i], axis[2 * d])

    def relay_a(i, d):
        return relay(ag_hbm, (ra_s, ra_r), i, z, c, zs, d)

    def g_pair(d):
        here = gg_hbm.at[y, 1 - x]
        return remote(here, here, gp_s.at[d], gp_r.at[d], ys[2 * d])

    def g_far(e, d):
        half = OUT // 2
        here = gg_hbm.at[(y + 3 - 2 * d) % 4, e, :, d * half : (d + 1) * half]
        return remote(here, here, gf_s.at[e, d], gf_r.at[e, d], ys[2 * d])

    a_loads = [
        pltpu.make_async_copy(ag_hbm.at[i // 2, i % 2], inr.at[i * 64 : (i + 1) * 64], al_sem.at[i]) for i in range(8)
    ]

    def pack(k):
        there = (y + k) % 4
        cp = pltpu.make_async_copy(gg_hbm.at[there], gst.at[k % 2], gl_sem.at[k % 2])
        cp.start()
        cp.wait()
        for b in range(4):
            cols = slice(b * GK, (b + 1) * GK)
            v = jnp.concatenate([gst[k % 2, 0, :, cols], gst[k % 2, 1, :, cols]], axis=0)
            ogt[pl.ds(pl.multiple_of(b * RZ + there * SEG, 16), SEG), 0:GK] = v

    def between(s, lo, n):
        return jnp.logical_and(s >= lo, s < lo + n)

    def background(s):
        @pl.when(s == 1)
        def _():
            for cp in a_sends:
                cp.wait()

        @pl.when(s == G_PAIR)
        def _():
            g_own.wait()
            for d in range(2):
                g_pair(d).start()

        @pl.when(s == G_PACK)
        def _():
            own_g.wait()
            pack(0)

        @pl.when(between(s, 1, A_SLICES // 2))
        def _():
            relay_a(2 * (s - 1), 0).start()
            relay_a(2 * (s - 1) + 1, 1).start()

        @pl.when(between(s, 3, A_SLICES // 2))
        def _():
            relay_a(2 * (s - 3), 0).wait()
            relay_a(2 * (s - 3) + 1, 1).wait()

        @pl.when(s == 3 + A_SLICES // 2)
        def _():
            own_a.wait()
            a_fwd.start()

        @pl.when(s == 5 + A_SLICES // 2)
        def _():
            a_fwd.wait()
            for cp in a_loads:
                cp.start()

    part = HALF // 6

    def og_load(i):
        return pltpu.make_async_copy(
            og_ref.at[:, pl.ds(mine + i * part, part)], inb.at[i % 2, :, 0:part], ld_sem.at[i % 2]
        )

    og_load(0).start()
    for i in range(6):
        if i < 5:
            og_load(i + 1).start()
        og_load(i).wait()
        for j in range(part // 128):
            ogt[i * part + j * 128 : i * part + (j + 1) * 128, 0:TOK] = inb[i % 2, :, j * 128 : (j + 1) * 128].T
    in_load(0).start()
    og_x.wait()
    in_x(1).start()

    def turn_r(j, _):
        lanes = pl.ds(pl.multiple_of(j * 128, 128), 128)
        ogt[pl.ds(pl.multiple_of(j * 128, 128), 128), TOK : 2 * TOK] = ogr[:, lanes].T
        return 0

    lax.fori_loop(0, HALF // 128, turn_r, 0)

    first, second = (z, y), (y, z)
    stride1, stride2 = (RZ, SEG), (SEG, RZ)
    axis1, axis2 = (zs, ys), (ys, zs)

    def near(k, d):
        return (k + 1) % 4 if d == 0 else (k + 3) % 4

    def rows(t, k, j):
        return pl.ds(pl.multiple_of(k * stride1[t] + j * stride2[t], 16), SEG)

    def ch(s, t):
        return 2 * s + t

    def send_a(s, t, d):
        return remote(s1.at[t, s % 2, d, 0], r1a.at[ch(s, t), d], s1_sem.at[t, s % 2], r1_sem.at[ch(s, t), 0], axis1[t][2 * d])

    def send_bc(s, t, d):
        return remote(s1.at[t, s % 2, d, pl.ds(1, 2)], r1bc.at[ch(s, t), d], s1_sem.at[t, s % 2], r1_sem.at[ch(s, t), 1], axis1[t][2 * d])

    def send_half(s, t, d, h):
        return remote(s1.at[t, s % 2, d, 1 + h], r1bc.at[ch(s, t), d, h], s1_sem.at[t, s % 2], r1_sem.at[ch(s, t), 1], axis1[t][2 * d])

    def send_2a(s, t, d):
        if t == 0:
            half = ROWHALF[d]
            return remote(m2.at[s % 2, d, half], q2a.at[s, half], s2_sem.at[t, s % 2], r2_sem.at[ch(s, t), 0], axis2[t][2 * d])
        return remote(s2.at[s % 2, d, 0], r2a.at[s, d], s2_sem.at[t, s % 2], r2_sem.at[ch(s, t), 0], axis2[t][2 * d])

    def send_2bc(s, t, d):
        if t == 0:
            return remote(m2.at[s % 2, 2 + d], q2bc.at[s, d], s2_sem.at[t, s % 2], r2_sem.at[ch(s, t), 1], axis2[t][2 * d])
        return remote(s2.at[s % 2, d, pl.ds(1, 2)], r2bc.at[s, d], s2_sem.at[t, s % 2], r2_sem.at[ch(s, t), 1], axis2[t][2 * d])

    def far_2(s, t):
        if t == 0:
            return [remote(m2.at[s % 2, 0], q2a.at[s], s2_sem.at[t, s % 2], r2_sem.at[ch(s, t), 0], ys[1])]
        return [
            remote(s2.at[s % 2, d, 0], r2a.at[s, d], s2_sem.at[t, s % 2], r2_sem.at[ch(s, t), 0], zs[1]) for d in range(2)
        ]

    def far_y(s, t):
        here = xg.at[pl.ds(pl.multiple_of(y * SEG, 16), SEG), tile(s, t)]
        return remote(here, here, yg_s.at[t, s % 2], yg_r.at[ch(s, t), 1], ys[1])

    def at_last(s, f, g):
        pl.when(s == STEPS - 1)(f)
        pl.when(s < STEPS - 1)(g)

    def send_x(s, t):
        if t == 0:
            return remote(mx.at[s % 2], qx.at[s], x_s.at[t, s % 2], x_r.at[ch(s, t)], xpeer)
        return remote(sx.at[s % 2], rx.at[s], x_s.at[t, s % 2], x_r.at[ch(s, t)], xpeer)

    def tile(s, t):
        return pl.ds(pl.multiple_of(ch(s, t) * W + x * COLS, COLS), COLS)

    def send_y(s, t, d):
        here = xg.at[pl.ds(pl.multiple_of(y * SEG, 16), SEG), tile(s, t)]
        return remote(here, here, yg_s.at[t, s % 2], yg_r.at[ch(s, t), 0], ys[2 * d])

    def relay_y(s, t):
        behind = near(y, 1 - t)
        here = xg.at[pl.ds(pl.multiple_of(behind * SEG, 16), SEG), tile(s, t)]
        return remote(here, here, yg_s.at[t, s % 2], yg_r.at[ch(s, t), 1], ys[2 * t])

    def send_fw(s, t, k):
        here = xg.at[pl.ds(pl.multiple_of((y // 2 + k) % 2 * (2 * SEG), 16), 2 * SEG), tile(s, t)]
        return remote(here, here, fw_s.at[ch(s, t)], fw_r.at[ch(s, t)], xpeer)

    def arrived(ref, sem):
        pltpu.make_async_copy(ref, ref, sem).wait()

    def fetch(s):
        in_load(s).wait()
        in_x(s).wait()

        @pl.when(s + 1 < STEPS)
        def _():
            in_load(s + 1).start()

        @pl.when(s + 2 < STEPS)
        def _():
            in_x(s + 2).start()

    def compute(s, ts):
        p = s % 2
        for t in ts:
            b_own = inb[p, :, t * W : (t + 1) * W]
            b_other = inr[:, pl.ds(pl.multiple_of(ch(s, t) * W, W), W)]

            def block(i, _):
                r = pl.ds(pl.multiple_of(i * RZ, 16), RZ)
                v = jnp.dot(ogt[r, 0:TOK], b_own, preferred_element_type=F32)
                v = v + jnp.dot(ogt[r, TOK : 2 * TOK], b_other, preferred_element_type=F32)
                acc[t, p, 0, r, :] = v[:, :COLS]
                acc[t, p, 1, r, :] = v[:, COLS:]
                return 0

            lax.fori_loop(0, NZ, block, 0)

    def send_first(s, t):
        p, m = s % 2, first[t]
        for d in range(2):
            for j in range(4):
                s1[t, p, d, 0, j] = acc[t, p, d, rows(t, (m + 2) % 4, j), :].astype(BF)
            send_a(s, t, d).start()
        for d in range(2):
            for j in range(4):
                s1[t, p, d, 2 - d, j] = acc[t, p, 1 - d, rows(t, near(m, d), j), :].astype(BF)

            @pl.when(s == STEPS - 1)
            def _(d=d):
                send_half(s, t, d, 1 - d).start()

    def pass_on(s, t):
        p = s % 2
        arrived(r1a.at[ch(s, t)], r1_sem.at[ch(s, t), 0])
        for d in range(2):
            for j in range(4):
                v = acc[t, p, d, rows(t, near(first[t], d), j), :] + r1a[ch(s, t), d, j].astype(F32)
                s1[t, p, d, 1 + d, j] = v.astype(BF)

            @pl.when(s == STEPS - 1)
            def _(d=d):
                send_half(s, t, d, d).start()

            @pl.when(s < STEPS - 1)
            def _(d=d):
                send_bc(s, t, d).start()

    def sum_first0(s):
        p = s % 2
        arrived(r1bc.at[ch(s, 0)], r1_sem.at[ch(s, 0), 1])

        def summed(h, j):
            v = acc[0, p, h, rows(0, z, j), :]
            return v + r1bc[ch(s, 0), 0, h, j].astype(F32) + r1bc[ch(s, 0), 1, h, j].astype(F32)

        for j in range(4):
            mx[p, j] = summed(1 - x, j).astype(BF)
        send_x(s, 0).start()
        for j in range(4):
            sums0[p, j] = summed(x, j)
        arrived(s1.at[0, p], s1_sem.at[0, p])

    def second0(s):
        p = s % 2
        send_x(s, 0).wait()
        for j in range(4):
            sums0[p, j] = sums0[p, j] + qx[s, j].astype(F32)
        far = sums0[p, (y + 2) % 4].astype(BF)
        for d in range(2):
            m2[p, d] = far

        def direct():
            for d in range(2):
                m2[p, 2 + d] = sums0[p, near(y, d)].astype(BF)
                send_2bc(s, 0, d).start()
            for cp in far_2(s, 0):
                cp.start()

        def relayed():
            for d in range(2):
                send_2a(s, 0, d).start()
            for d in range(2):
                half = ROWHALF[1 - d]
                m2[p, 2 + d, half, :] = sums0[p, near(y, d), half, :].astype(BF)

        at_last(s, direct, relayed)

    def pass_on_second0(s):
        p = s % 2
        arrived(q2a.at[s], r2_sem.at[ch(s, 0), 0])

        @pl.when(s < STEPS - 1)
        def _():
            for d in range(2):
                half = ROWHALF[d]
                v = sums0[p, near(y, d), half, :] + q2a[s, half, :].astype(F32)
                m2[p, 2 + d, half, :] = v.astype(BF)
                send_2bc(s, 0, d).start()

    def finish0(s):
        p = s % 2
        arrived(q2bc.at[s], r2_sem.at[ch(s, 0), 1])
        v = sums0[p, y] + q2bc[s, 0].astype(F32) + q2bc[s, 1].astype(F32)
        v = v + jnp.where(s == STEPS - 1, q2a[s].astype(F32), 0.0)
        xg[pl.ds(pl.multiple_of(y * SEG, 16), SEG), tile(s, 0)] = v.astype(BF)
        for d in range(2):
            send_y(s, 0, d).start()
        pl.when(s == STEPS - 1)(lambda: far_y(s, 0).start())
        arrived(m2.at[p, pl.ds(1, 3)], s2_sem.at[0, p])

    def sum_first1(s):
        t, p, m = 1, s % 2, z
        arrived(r1bc.at[ch(s, t)], r1_sem.at[ch(s, t), 1])
        for h in range(2):
            for j in range(4):
                v = acc[t, p, h, rows(t, y, j), :]
                sums[p, h, j] = v + r1bc[ch(s, t), 0, h, j].astype(F32) + r1bc[ch(s, t), 1, h, j].astype(F32)
        for d in range(2):
            s2[p, d, 0] = sums[p, d, (m + 2) % 4].astype(BF)
        for d in range(2):
            s2[p, d, 2 - d] = sums[p, 1 - d, near(m, d)].astype(BF)

        def direct():
            for d in range(2):
                s2[p, d, 1 + d] = sums[p, d, near(m, d)].astype(BF)
                send_2bc(s, t, d).start()
            for cp in far_2(s, t):
                cp.start()

        def relayed():
            for d in range(2):
                send_2a(s, t, d).start()

        at_last(s, direct, relayed)
        arrived(s1.at[t, p], s1_sem.at[t, p])

    def pass_on_second1(s):
        p = s % 2
        arrived(r2a.at[s], r2_sem.at[ch(s, 1), 0])

        @pl.when(s < STEPS - 1)
        def _():
            for d in range(2):
                v = sums[p, d, near(z, d)] + r2a[s, d].astype(F32)
                s2[p, d, 1 + d] = v.astype(BF)
                send_2bc(s, 1, d).start()

    def sum_second1(s):
        p = s % 2
        arrived(r2bc.at[s], r2_sem.at[ch(s, 1), 1])
        for h in range(2):
            v = sums[p, h, z] + r2bc[s, 0, h].astype(F32) + r2bc[s, 1, h].astype(F32)
            tot[p, h] = v + jnp.where(s == STEPS - 1, r2a[s, h].astype(F32), 0.0)
        sx[p] = tot[p, 1 - x]
        send_x(s, 1).start()
        arrived(s2.at[p], s2_sem.at[1, p])

    def finish1(s):
        send_x(s, 1).wait()
        v = tot[s % 2, x] + rx[s]
        xg[pl.ds(pl.multiple_of(y * SEG, 16), SEG), tile(s, 1)] = v.astype(BF)
        for d in range(2):
            send_y(s, 1, d).start()
        pl.when(s == STEPS - 1)(lambda: far_y(s, 1).start())

    def relay_tiles(s, t):
        arrived(xg.at[pl.ds(0, 2 * SEG), tile(s, t)], yg_r.at[ch(s, t), 0])
        pl.when(s < STEPS - 1)(lambda: relay_y(s, t).start())
        send_fw(s, t, 0).start()

    def forward(s, t):
        arrived(xg.at[pl.ds(0, SEG), tile(s, t)], yg_r.at[ch(s, t), 1])
        send_fw(s, t, 1).start()
        arrived(xg.at[pl.ds(0, 3 * SEG), tile(s, t)], yg_s.at[t, s % 2])

    def complete(s, t):
        whole = xg.at[:, tile(s, t)]
        arrived(whole, fw_s.at[ch(s, t)])
        arrived(whole, fw_r.at[ch(s, t)])

    def both(f):
        def g(s):
            for t in range(2):
                f(s, t)

        return g

    stages = [
        (2, sum_first0),
        (2, sum_first1),
        (1, both(pass_on)),
        (3, pass_on_second0),
        (3, sum_second1),
        (4, both(relay_tiles)),
        (0, fetch),
        (0, lambda s: compute(s, (0,))),
        (2, pass_on_second1),
        (0, lambda s: send_first(s, 0)),
        (0, lambda s: compute(s, (1,))),
        (0, lambda s: send_first(s, 1)),
        (3, finish0),
        (2, second0),
        (3, finish1),
        (6, both(complete)),
        (4, both(forward)),
    ]

    def step(s, _):
        for lag, stage in stages:

            @pl.when(jnp.logical_and(s >= lag, s < STEPS + lag))
            def _(lag=lag, stage=stage):
                stage(s - lag)

        background(s)
        return 0

    lax.fori_loop(0, LAST, step, 0)
    for cp in a_loads:
        cp.wait()

    def send_r(q, d):
        here = rg.at[q, my_rows]
        return remote(here, here, z_s.at[q, d], z_r.at[q, d], zs[2 * d])

    def relay_r(q):
        d = q % 2
        behind = near(z, 1 - d)
        here = rg.at[q, pl.ds(pl.multiple_of(c * HALF + behind * RZ, 16), RZ)]
        return remote(here, here, z_s.at[q, 2], z_r.at[q, 2], zs[2 * d])

    def send_core(q):
        here = rg.at[q, core_rows]
        return remote(here, here, c_s.at[q], c_r.at[q], core)

    def utile(q):
        return pl.ds(pl.multiple_of(((q * 4 + y) * 2 + x) * COLS, COLS), COLS)

    def urows(owner):
        return pl.ds(pl.multiple_of(owner * (OUT // 64), 8), OUT // 64)

    def send_u(q, i):
        k, e = offs[i]
        owner = ((y + k) % 4) * 2 + (x + e) % 2
        return remote(acc.at[q // 2, q % 2, 0, urows(owner)], uo.at[:, utile(q)], u_s.at[q, i], u_r.at[q, i], yx[i])

    def right(q):
        v = lax.dot_general(
            xg[...], inr[q * COLS : (q + 1) * COLS, :], (((1,), (1,)), ((), ())), preferred_element_type=F32
        )
        rg[q, my_rows, :] = v.astype(BF)
        for d in range(2):
            send_r(q, d).start()

    def pass_right(q):
        for d in range(2):
            send_r(q, d).wait()
        relay_r(q).start()

    def share_right(q):
        relay_r(q).wait()
        send_core(q).start()

    def update(q):
        send_core(q).wait()
        v = jnp.zeros((RZ, COLS), F32)
        for b in range(4):
            v = v + jnp.dot(
                ogt[b * RZ : (b + 1) * RZ, 0:GK], rg[q, b * GK : (b + 1) * GK, :], preferred_element_type=F32
            )
        acc[q // 2, q % 2, 0, 0:RZ, :] = v
        uo[:, utile(q)] = acc[q // 2, q % 2, 0, urows(y * 2 + x), :]
        for i in range(7):
            send_u(q, i).start()

    right(0)
    right(1)
    for cp in g_sends:
        cp.wait()
    for d in range(2):
        g_pair(d).wait()
    for e in range(2):
        for d in range(2):
            g_far(e, d).start()
    pass_right(0)
    right(2)
    pass_right(1)
    pack(1)
    right(3)
    share_right(0)
    pass_right(2)
    pack(3)
    share_right(1)
    pass_right(3)
    for e in range(2):
        for d in range(2):
            g_far(e, d).wait()
    pack(2)
    update(0)
    share_right(2)
    update(1)
    share_right(3)
    update(2)
    update(3)
    for q in range(4):
        for i in range(7):
            send_u(q, i).wait()
    cp = pltpu.make_async_copy(uo, u_out, load_sem.at[0])
    cp.start()
    cp.wait()


def reduce_call(inputs, out_grad, a_inverse, g_inverse):
    anyspace = pl.BlockSpec(memory_space=pl.ANY)
    n = 2 * STEPS
    dma = pltpu.SemaphoreType.DMA
    return pl.pallas_call(
        reduce_kernel,
        out_shape=[
            jax.ShapeDtypeStruct((OUT // 64, IN), F32),
            jax.ShapeDtypeStruct((4, 2, IN // 64, IN), BF),
            jax.ShapeDtypeStruct((4, 2, OUT // 64, OUT), BF),
        ],
        in_specs=[anyspace] * 4,
        out_specs=[anyspace] * 3,
        scratch_shapes=[
            pltpu.VMEM((HALF, 2 * TOK), BF),
            pltpu.VMEM((TOK, HALF), BF),
            pltpu.VMEM((2, TOK, 2 * W), BF),
            pltpu.VMEM((TOK, IN), BF),
            pltpu.VMEM((2, 2, 2, HALF, COLS), F32),
            pltpu.VMEM((2, 2, 2, 3, 4, SEG, COLS), BF),
            pltpu.VMEM((n, 2, 4, SEG, COLS), BF),
            pltpu.VMEM((n, 2, 2, 4, SEG, COLS), BF),
            pltpu.VMEM((2, 4, SEG, COLS), F32),
            pltpu.VMEM((2, 4, SEG, COLS), BF),
            pltpu.VMEM((STEPS, 4, SEG, COLS), BF),
            pltpu.VMEM((2, 4, SEG, COLS), BF),
            pltpu.VMEM((STEPS, SEG, COLS), BF),
            pltpu.VMEM((STEPS, 2, SEG, COLS), BF),
            pltpu.VMEM((2, 2, 4, SEG, COLS), F32),
            pltpu.VMEM((2, 2, 3, SEG, COLS), BF),
            pltpu.VMEM((STEPS, 2, SEG, COLS), BF),
            pltpu.VMEM((STEPS, 2, 2, SEG, COLS), BF),
            pltpu.VMEM((2, 2, SEG, COLS), F32),
            pltpu.VMEM((2, SEG, COLS), F32),
            pltpu.VMEM((STEPS, SEG, COLS), F32),
            pltpu.VMEM((RZ, IN), BF),
            dma((1,)),
            dma((2,)),
            dma((1 + STEPS,)),
            dma((1 + STEPS,)),
            dma((2, 2)),
            dma((n, 2)),
            dma((2, 2)),
            dma((n, 2)),
            dma((2, 2)),
            dma((n,)),
            dma((2, 2)),
            dma((n, 2)),
            dma((n,)),
            dma((n,)),
            dma((6,)),
            dma((6,)),
            dma((A_SLICES,)),
            dma((A_SLICES,)),
            dma((2,)),
            dma((2,)),
            dma((2, 2)),
            dma((2, 2)),
            dma((2,)),
            dma((8,)),
            dma((2,)),
            pltpu.VMEM((2, 2, OUT // 64, OUT), BF),
            pltpu.VMEM((4, OUT, COLS), BF),
            pltpu.VMEM((OUT // 64, IN), F32),
            dma((4, 3)),
            dma((4, 3)),
            dma((4,)),
            dma((4,)),
            dma((4, 7)),
            dma((4, 7)),
        ],
        compiler_params=pltpu.CompilerParams(
            collective_id=0, has_side_effects=True, vmem_limit_bytes=63 * 1024 * 1024
        ),
        cost_estimate=pl.CostEstimate(flops=29_400_000_000, bytes_accessed=40_000_000, transcendentals=0),
        name="kfac_update",
    )(inputs, out_grad, a_inverse, g_inverse)


def per_device(inputs, out_grad, a_inverse, g_inverse, weights, momentum):
    update = reduce_call(inputs, out_grad, a_inverse, g_inverse)[0]
    new_momentum = 0.9 * momentum + update
    new_weights = weights - 0.5 * new_momentum
    return (new_weights, new_momentum)


def solution(mesh):
    spec = P(("pipe", "dp"), None)
    return jax.shard_map(
        per_device, mesh=mesh, in_specs=(spec,) * 6, out_specs=(spec, spec), check_vma=False
    )
```

```python
import functools

import jax
import jax.numpy as jnp
from jax import lax
from jax.experimental import pallas as pl
from jax.experimental.pallas import tpu as pltpu
from jax.sharding import PartitionSpec as P

BF = jnp.bfloat16
F32 = jnp.float32
MESH = pl.DeviceIdType.MESH
NZ, NY = 4, 4
IN, OUT, TOK = 4096, 4608, 640
HALF = OUT // 2
RZ = HALF // NZ
SEG = RZ // NY
W = 256
STEPS = IN // (2 * W)
COLS = 128
ROWHALF = (slice(0, 80), slice(80, 144))
LAST = STEPS + 6
G_PAIR, G_PACK = 11, 12
GK = OUT // 4
SLICE = 512
A_SLICES = IN // SLICE


def coords():
    d = lax.axis_index("dp")
    return d // 16, (d // 4) % 4, (d // 2) % 2, d % 2


def dev(z, y, x, c):
    return {"dp": ((z * 4 + y) * 2 + x) * 2 + c}


def remote(src, dst, ssem, rsem, to):
    return pltpu.make_async_remote_copy(
        src_ref=src, dst_ref=dst, send_sem=ssem, recv_sem=rsem, device_id=to, device_id_type=MESH
    )


def greet(peers):
    barrier = pltpu.get_barrier_semaphore()
    for p in peers:
        pl.semaphore_signal(barrier, inc=1, device_id=p, device_id_type=MESH)
    pl.semaphore_wait(barrier, len(peers))


def reduce_kernel(
    in_ref, og_ref, a_ref, g_ref, u_out, ag_hbm, gg_hbm,
    ogt, ogr, inb, inr, acc, s1, r1a, r1bc,
    sums0, mx, qx, m2, q2a, q2bc, sums, s2, r2a, r2bc, tot, sx, rx, xg,
    ld_sem, pair_s, pair_r, s1_sem, r1_sem, s2_sem, r2_sem, x_s, x_r, yg_s, yg_r, fw_s, fw_r, ag_s, ag_r, ra_s, ra_r, gp_s, gp_r, gf_s, gf_r, own_sem,
    al_sem, gl_sem, st_sem, gst, rg, uo, z_s, z_r, c_s, c_r, u_s, u_r,
):
    z, y, x, c = coords()
    core = dev(z, y, x, 1 - c)
    xpeer = dev(z, y, 1 - x, c)
    zs = [dev((z + k) % 4, y, x, c) for k in (1, 2, 3)]
    ys = [dev(z, (y + k) % 4, x, c) for k in (1, 2, 3)]
    offs = [(k, e) for k in range(4) for e in range(2) if (k, e) != (0, 0)]
    yx = [dev(z, (y + k) % 4, (x + e) % 2, c) for k, e in offs]
    greet([core] + zs + yx)
    my_rows = pl.ds(pl.multiple_of(c * HALF + z * RZ, 16), RZ)
    core_rows = pl.ds(pl.multiple_of(c * HALF, 16), HALF)
    other_rows = pl.ds(pl.multiple_of((1 - c) * HALF, 16), HALF)

    other = pl.multiple_of((1 - c) * HALF, 128)
    mine = pl.multiple_of(c * HALF, 128)

    og_x = remote(og_ref.at[:, pl.ds(other, HALF)], ogr, pair_s.at[0], pair_r.at[0], core)
    og_x.start()

    def in_x(s):
        cols = pl.ds(pl.multiple_of(s * 2 * W, 2 * W), 2 * W)
        return remote(in_ref.at[:, cols], inr.at[:, cols], pair_s.at[1 + s], pair_r.at[1 + s], core)

    in_x(0).start()

    def in_load(s):
        cols = pl.ds(pl.multiple_of(s * 2 * W, 2 * W), 2 * W)
        return pltpu.make_async_copy(in_ref.at[:, cols], inb.at[s % 2], ld_sem.at[s % 2])


    own_a = pltpu.make_async_copy(a_ref, ag_hbm.at[z, c], own_sem.at[0])
    own_g = pltpu.make_async_copy(g_ref, gg_hbm.at[y, x], own_sem.at[1])
    own_a.start()
    own_g.start()
    a_sends = [remote(a_ref, ag_hbm.at[z, c], ag_s.at[k], ag_r.at[k], zs[2 * k]) for k in range(2)]
    g_sends = [remote(g_ref, gg_hbm.at[y, x], ag_s.at[2 + k], ag_r.at[2 + k], ys[2 * k]) for k in range(2)]
    a_fwd = remote(ag_hbm.at[:, c], ag_hbm.at[:, c], ag_s.at[4], ag_r.at[4], core)
    g_own = remote(g_ref, gg_hbm.at[y, x], ag_s.at[5], ag_r.at[5], xpeer)
    for cp in a_sends + g_sends + [g_own]:
        cp.start()

    def relay(out, sem, i, k, other_k, axis, d):
        cols = pl.ds(pl.multiple_of(i * SLICE, SLICE), SLICE)
        from_k = (k + 3) % 4 if d == 0 else (k + 1) % 4
        here = out.at[from_k, other_k, :, cols]
        return remote(here, here, sem[0].at[i], sem[1].at[i], axis[2 * d])

    def relay_a(i, d):
        return relay(ag_hbm, (ra_s, ra_r), i, z, c, zs, d)

    def g_pair(d):
        here = gg_hbm.at[y, 1 - x]
        return remote(here, here, gp_s.at[d], gp_r.at[d], ys[2 * d])

    def g_far(e, d):
        half = OUT // 2
        here = gg_hbm.at[(y + 3 - 2 * d) % 4, e, :, d * half : (d + 1) * half]
        return remote(here, here, gf_s.at[e, d], gf_r.at[e, d], ys[2 * d])

    a_loads = [
        pltpu.make_async_copy(ag_hbm.at[i // 2, i % 2], inr.at[i * 64 : (i + 1) * 64], al_sem.at[i]) for i in range(8)
    ]

    def pack(k):
        there = (y + k) % 4
        cp = pltpu.make_async_copy(gg_hbm.at[there], gst.at[k % 2], gl_sem.at[k % 2])
        cp.start()
        cp.wait()
        for b in range(4):
            cols = slice(b * GK, (b + 1) * GK)
            v = jnp.concatenate([gst[k % 2, 0, :, cols], gst[k % 2, 1, :, cols]], axis=0)
            ogt[pl.ds(pl.multiple_of(b * RZ + there * SEG, 16), SEG), 0:GK] = v

    def between(s, lo, n):
        return jnp.logical_and(s >= lo, s < lo + n)

    def background(s):
        @pl.when(s == 1)
        def _():
            for cp in a_sends:
                cp.wait()

        @pl.when(s == G_PAIR)
        def _():
            g_own.wait()
            for d in range(2):
                g_pair(d).start()

        @pl.when(s == G_PACK)
        def _():
            own_g.wait()
            pack(0)

        @pl.when(between(s, 1, A_SLICES // 2))
        def _():
            relay_a(2 * (s - 1), 0).start()
            relay_a(2 * (s - 1) + 1, 1).start()

        @pl.when(between(s, 3, A_SLICES // 2))
        def _():
            relay_a(2 * (s - 3), 0).wait()
            relay_a(2 * (s - 3) + 1, 1).wait()

        @pl.when(s == 3 + A_SLICES // 2)
        def _():
            own_a.wait()
            a_fwd.start()

        @pl.when(s == 5 + A_SLICES // 2)
        def _():
            a_fwd.wait()
            for cp in a_loads:
                cp.start()

    part = HALF // 6

    def og_load(i):
        return pltpu.make_async_copy(
            og_ref.at[:, pl.ds(mine + i * part, part)], inb.at[i % 2, :, 0:part], ld_sem.at[i % 2]
        )

    og_load(0).start()
    for i in range(6):
        if i < 5:
            og_load(i + 1).start()
        og_load(i).wait()
        for j in range(part // 128):
            ogt[i * part + j * 128 : i * part + (j + 1) * 128, 0:TOK] = inb[i % 2, :, j * 128 : (j + 1) * 128].T
    in_load(0).start()
    og_x.wait()
    in_x(1).start()

    def turn_r(j, _):
        lanes = pl.ds(pl.multiple_of(j * 128, 128), 128)
        ogt[pl.ds(pl.multiple_of(j * 128, 128), 128), TOK : 2 * TOK] = ogr[:, lanes].T
        return 0

    lax.fori_loop(0, HALF // 128, turn_r, 0)

    first, second = (z, y), (y, z)
    stride1, stride2 = (RZ, SEG), (SEG, RZ)
    axis1, axis2 = (zs, ys), (ys, zs)

    def near(k, d):
        return (k + 1) % 4 if d == 0 else (k + 3) % 4

    def rows(t, k, j):
        return pl.ds(pl.multiple_of(k * stride1[t] + j * stride2[t], 16), SEG)

    def ch(s, t):
        return 2 * s + t

    def send_a(s, t, d):
        return remote(s1.at[t, s % 2, d, 0], r1a.at[ch(s, t), d], s1_sem.at[t, s % 2], r1_sem.at[ch(s, t), 0], axis1[t][2 * d])

    def send_bc(s, t, d):
        return remote(s1.at[t, s % 2, d, pl.ds(1, 2)], r1bc.at[ch(s, t), d], s1_sem.at[t, s % 2], r1_sem.at[ch(s, t), 1], axis1[t][2 * d])

    def send_half(s, t, d, h):
        return remote(s1.at[t, s % 2, d, 1 + h], r1bc.at[ch(s, t), d, h], s1_sem.at[t, s % 2], r1_sem.at[ch(s, t), 1], axis1[t][2 * d])

    def send_2a(s, t, d):
        if t == 0:
            half = ROWHALF[d]
            return remote(m2.at[s % 2, d, half], q2a.at[s, half], s2_sem.at[t, s % 2], r2_sem.at[ch(s, t), 0], axis2[t][2 * d])
        return remote(s2.at[s % 2, d, 0], r2a.at[s, d], s2_sem.at[t, s % 2], r2_sem.at[ch(s, t), 0], axis2[t][2 * d])

    def send_2bc(s, t, d):
        if t == 0:
            return remote(m2.at[s % 2, 2 + d], q2bc.at[s, d], s2_sem.at[t, s % 2], r2_sem.at[ch(s, t), 1], axis2[t][2 * d])
        return remote(s2.at[s % 2, d, pl.ds(1, 2)], r2bc.at[s, d], s2_sem.at[t, s % 2], r2_sem.at[ch(s, t), 1], axis2[t][2 * d])

    def far_2(s, t):
        if t == 0:
            return [remote(m2.at[s % 2, 0], q2a.at[s], s2_sem.at[t, s % 2], r2_sem.at[ch(s, t), 0], ys[1])]
        return [
            remote(s2.at[s % 2, d, 0], r2a.at[s, d], s2_sem.at[t, s % 2], r2_sem.at[ch(s, t), 0], zs[1]) for d in range(2)
        ]

    def far_y(s, t):
        here = xg.at[pl.ds(pl.multiple_of(y * SEG, 16), SEG), tile(s, t)]
        return remote(here, here, yg_s.at[t, s % 2], yg_r.at[ch(s, t), 1], ys[1])

    def at_last(s, f, g):
        pl.when(s == STEPS - 1)(f)
        pl.when(s < STEPS - 1)(g)

    def send_x(s, t):
        if t == 0:
            return remote(mx.at[s % 2], qx.at[s], x_s.at[t, s % 2], x_r.at[ch(s, t)], xpeer)
        return remote(sx.at[s % 2], rx.at[s], x_s.at[t, s % 2], x_r.at[ch(s, t)], xpeer)

    def tile(s, t):
        return pl.ds(pl.multiple_of(ch(s, t) * W + x * COLS, COLS), COLS)

    def send_y(s, t, d):
        here = xg.at[pl.ds(pl.multiple_of(y * SEG, 16), SEG), tile(s, t)]
        return remote(here, here, yg_s.at[t, s % 2], yg_r.at[ch(s, t), 0], ys[2 * d])

    def relay_y(s, t):
        behind = near(y, 1 - t)
        here = xg.at[pl.ds(pl.multiple_of(behind * SEG, 16), SEG), tile(s, t)]
        return remote(here, here, yg_s.at[t, s % 2], yg_r.at[ch(s, t), 1], ys[2 * t])

    def send_fw(s, t, k):
        here = xg.at[pl.ds(pl.multiple_of((y // 2 + k) % 2 * (2 * SEG), 16), 2 * SEG), tile(s, t)]
        return remote(here, here, fw_s.at[ch(s, t)], fw_r.at[ch(s, t)], xpeer)

    def arrived(ref, sem):
        pltpu.make_async_copy(ref, ref, sem).wait()

    def fetch(s):
        in_load(s).wait()
        in_x(s).wait()

        @pl.when(s + 1 < STEPS)
        def _():
            in_load(s + 1).start()

        @pl.when(s + 2 < STEPS)
        def _():
            in_x(s + 2).start()

    def compute(s, ts):
        p = s % 2
        for t in ts:
            b_own = inb[p, :, t * W : (t + 1) * W]
            b_other = inr[:, pl.ds(pl.multiple_of(ch(s, t) * W, W), W)]

            def block(i, _):
                r = pl.ds(pl.multiple_of(i * RZ, 16), RZ)
                v = jnp.dot(ogt[r, 0:TOK], b_own, preferred_element_type=F32)
                v = v + jnp.dot(ogt[r, TOK : 2 * TOK], b_other, preferred_element_type=F32)
                acc[t, p, 0, r, :] = v[:, :COLS]
                acc[t, p, 1, r, :] = v[:, COLS:]
                return 0

            lax.fori_loop(0, NZ, block, 0)

    def send_first(s, t):
        p, m = s % 2, first[t]
        for d in range(2):
            for j in range(4):
                s1[t, p, d, 0, j] = acc[t, p, d, rows(t, (m + 2) % 4, j), :].astype(BF)
            send_a(s, t, d).start()
        for d in range(2):
            for j in range(4):
                s1[t, p, d, 2 - d, j] = acc[t, p, 1 - d, rows(t, near(m, d), j), :].astype(BF)

            @pl.when(s == STEPS - 1)
            def _(d=d):
                send_half(s, t, d, 1 - d).start()

    def pass_on(s, t):
        p = s % 2
        arrived(r1a.at[ch(s, t)], r1_sem.at[ch(s, t), 0])
        for d in range(2):
            for j in range(4):
                v = acc[t, p, d, rows(t, near(first[t], d), j), :] + r1a[ch(s, t), d, j].astype(F32)
                s1[t, p, d, 1 + d, j] = v.astype(BF)

            @pl.when(s == STEPS - 1)
            def _(d=d):
                send_half(s, t, d, d).start()

            @pl.when(s < STEPS - 1)
            def _(d=d):
                send_bc(s, t, d).start()

    def sum_first0(s):
        p = s % 2
        arrived(r1bc.at[ch(s, 0)], r1_sem.at[ch(s, 0), 1])

        def summed(h, j):
            v = acc[0, p, h, rows(0, z, j), :]
            return v + r1bc[ch(s, 0), 0, h, j].astype(F32) + r1bc[ch(s, 0), 1, h, j].astype(F32)

        for j in range(4):
            mx[p, j] = summed(1 - x, j).astype(BF)
        send_x(s, 0).start()
        for j in range(4):
            sums0[p, j] = summed(x, j)
        arrived(s1.at[0, p], s1_sem.at[0, p])

    def second0(s):
        p = s % 2
        send_x(s, 0).wait()
        for j in range(4):
            sums0[p, j] = sums0[p, j] + qx[s, j].astype(F32)
        far = sums0[p, (y + 2) % 4].astype(BF)
        for d in range(2):
            m2[p, d] = far

        def direct():
            for d in range(2):
                m2[p, 2 + d] = sums0[p, near(y, d)].astype(BF)
                send_2bc(s, 0, d).start()
            for cp in far_2(s, 0):
                cp.start()

        def relayed():
            for d in range(2):
                send_2a(s, 0, d).start()
            for d in range(2):
                half = ROWHALF[1 - d]
                m2[p, 2 + d, half, :] = sums0[p, near(y, d), half, :].astype(BF)

        at_last(s, direct, relayed)

    def pass_on_second0(s):
        p = s % 2
        arrived(q2a.at[s], r2_sem.at[ch(s, 0), 0])

        @pl.when(s < STEPS - 1)
        def _():
            for d in range(2):
                half = ROWHALF[d]
                v = sums0[p, near(y, d), half, :] + q2a[s, half, :].astype(F32)
                m2[p, 2 + d, half, :] = v.astype(BF)
                send_2bc(s, 0, d).start()

    def finish0(s):
        p = s % 2
        arrived(q2bc.at[s], r2_sem.at[ch(s, 0), 1])
        v = sums0[p, y] + q2bc[s, 0].astype(F32) + q2bc[s, 1].astype(F32)
        v = v + jnp.where(s == STEPS - 1, q2a[s].astype(F32), 0.0)
        xg[pl.ds(pl.multiple_of(y * SEG, 16), SEG), tile(s, 0)] = v.astype(BF)
        for d in range(2):
            send_y(s, 0, d).start()
        pl.when(s == STEPS - 1)(lambda: far_y(s, 0).start())
        arrived(m2.at[p, pl.ds(1, 3)], s2_sem.at[0, p])

    def sum_first1(s):
        t, p, m = 1, s % 2, z
        arrived(r1bc.at[ch(s, t)], r1_sem.at[ch(s, t), 1])
        for h in range(2):
            for j in range(4):
                v = acc[t, p, h, rows(t, y, j), :]
                sums[p, h, j] = v + r1bc[ch(s, t), 0, h, j].astype(F32) + r1bc[ch(s, t), 1, h, j].astype(F32)
        for d in range(2):
            s2[p, d, 0] = sums[p, d, (m + 2) % 4].astype(BF)
        for d in range(2):
            s2[p, d, 2 - d] = sums[p, 1 - d, near(m, d)].astype(BF)

        def direct():
            for d in range(2):
                s2[p, d, 1 + d] = sums[p, d, near(m, d)].astype(BF)
                send_2bc(s, t, d).start()
            for cp in far_2(s, t):
                cp.start()

        def relayed():
            for d in range(2):
                send_2a(s, t, d).start()

        at_last(s, direct, relayed)
        arrived(s1.at[t, p], s1_sem.at[t, p])

    def pass_on_second1(s):
        p = s % 2
        arrived(r2a.at[s], r2_sem.at[ch(s, 1), 0])

        @pl.when(s < STEPS - 1)
        def _():
            for d in range(2):
                v = sums[p, d, near(z, d)] + r2a[s, d].astype(F32)
                s2[p, d, 1 + d] = v.astype(BF)
                send_2bc(s, 1, d).start()

    def sum_second1(s):
        p = s % 2
        arrived(r2bc.at[s], r2_sem.at[ch(s, 1), 1])
        for h in range(2):
            v = sums[p, h, z] + r2bc[s, 0, h].astype(F32) + r2bc[s, 1, h].astype(F32)
            tot[p, h] = v + jnp.where(s == STEPS - 1, r2a[s, h].astype(F32), 0.0)
        sx[p] = tot[p, 1 - x]
        send_x(s, 1).start()
        arrived(s2.at[p], s2_sem.at[1, p])

    def finish1(s):
        send_x(s, 1).wait()
        v = tot[s % 2, x] + rx[s]
        xg[pl.ds(pl.multiple_of(y * SEG, 16), SEG), tile(s, 1)] = v.astype(BF)
        for d in range(2):
            send_y(s, 1, d).start()
        pl.when(s == STEPS - 1)(lambda: far_y(s, 1).start())

    def relay_tiles(s, t):
        arrived(xg.at[pl.ds(0, 2 * SEG), tile(s, t)], yg_r.at[ch(s, t), 0])
        pl.when(s < STEPS - 1)(lambda: relay_y(s, t).start())
        send_fw(s, t, 0).start()

    def forward(s, t):
        arrived(xg.at[pl.ds(0, SEG), tile(s, t)], yg_r.at[ch(s, t), 1])
        send_fw(s, t, 1).start()
        arrived(xg.at[pl.ds(0, 3 * SEG), tile(s, t)], yg_s.at[t, s % 2])

    def complete(s, t):
        whole = xg.at[:, tile(s, t)]
        arrived(whole, fw_s.at[ch(s, t)])
        arrived(whole, fw_r.at[ch(s, t)])

    def both(f):
        def g(s):
            for t in range(2):
                f(s, t)

        return g

    stages = [
        (2, sum_first0),
        (2, sum_first1),
        (1, both(pass_on)),
        (3, pass_on_second0),
        (3, sum_second1),
        (4, both(relay_tiles)),
        (0, fetch),
        (0, lambda s: compute(s, (0,))),
        (2, pass_on_second1),
        (0, lambda s: send_first(s, 0)),
        (0, lambda s: compute(s, (1,))),
        (0, lambda s: send_first(s, 1)),
        (3, finish0),
        (2, second0),
        (3, finish1),
        (6, both(complete)),
        (4, both(forward)),
    ]

    def step(s, _):
        for lag, stage in stages:

            @pl.when(jnp.logical_and(s >= lag, s < STEPS + lag))
            def _(lag=lag, stage=stage):
                stage(s - lag)

        background(s)
        return 0

    lax.fori_loop(0, LAST, step, 0)
    for cp in a_loads:
        cp.wait()

    def send_r(q, d):
        here = rg.at[q, my_rows]
        return remote(here, here, z_s.at[q, d], z_r.at[q, d], zs[2 * d])

    def relay_r(q):
        d = q % 2
        behind = near(z, 1 - d)
        here = rg.at[q, pl.ds(pl.multiple_of(c * HALF + behind * RZ, 16), RZ)]
        return remote(here, here, z_s.at[q, 2], z_r.at[q, 2], zs[2 * d])

    def send_core(q, k):
        here = rg.at[q, pl.ds(pl.multiple_of(c * HALF + ((z + k) % 4) * RZ, 16), RZ)]
        return remote(here, here, c_s.at[q], c_r.at[q], core)

    def utile(q):
        return pl.ds(pl.multiple_of(((q * 4 + y) * 2 + x) * COLS, COLS), COLS)

    def urows(owner):
        return pl.ds(pl.multiple_of(owner * (OUT // 64), 8), OUT // 64)

    def send_u(q, i):
        k, e = offs[i]
        owner = ((y + k) % 4) * 2 + (x + e) % 2
        return remote(acc.at[q // 2, q % 2, 0, urows(owner)], uo.at[:, utile(q)], u_s.at[q, i], u_r.at[q, i], yx[i])

    def right(q):
        v = lax.dot_general(
            xg[...], inr[q * COLS : (q + 1) * COLS, :], (((1,), (1,)), ((), ())), preferred_element_type=F32
        )
        rg[q, my_rows, :] = v.astype(BF)
        for d in range(2):
            send_r(q, d).start()
        send_core(q, 0).start()

    def pass_right(q):
        for d in range(2):
            send_r(q, d).wait()
        relay_r(q).start()
        send_core(q, 1).start()
        send_core(q, 3).start()

    def share_right(q):
        relay_r(q).wait()
        send_core(q, 2).start()

    def update(q):
        arrived(rg.at[q, core_rows], c_s.at[q])
        arrived(rg.at[q, other_rows], c_r.at[q])
        v = jnp.zeros((RZ, COLS), F32)
        for b in range(4):
            v = v + jnp.dot(
                ogt[b * RZ : (b + 1) * RZ, 0:GK], rg[q, b * GK : (b + 1) * GK, :], preferred_element_type=F32
            )
        acc[q // 2, q % 2, 0, 0:RZ, :] = v
        uo[:, utile(q)] = acc[q // 2, q % 2, 0, urows(y * 2 + x), :]
        for i in range(7):
            send_u(q, i).start()

    right(0)
    right(1)
    for cp in g_sends:
        cp.wait()
    for d in range(2):
        g_pair(d).wait()
    for e in range(2):
        for d in range(2):
            g_far(e, d).start()
    pass_right(0)
    right(2)
    pass_right(1)
    pack(1)
    right(3)
    share_right(0)
    pass_right(2)
    pack(3)
    share_right(1)
    pass_right(3)
    for e in range(2):
        for d in range(2):
            g_far(e, d).wait()
    pack(2)
    update(0)
    share_right(2)
    update(1)
    share_right(3)
    update(2)
    update(3)
    def store(q):
        cols = pl.ds(q * 8 * COLS, 8 * COLS)
        return pltpu.make_async_copy(uo.at[:, cols], u_out.at[:, cols], st_sem.at[q])

    for q in range(4):
        for i in range(7):
            send_u(q, i).wait()
        store(q).start()
    for q in range(4):
        store(q).wait()


def reduce_call(inputs, out_grad, a_inverse, g_inverse):
    anyspace = pl.BlockSpec(memory_space=pl.ANY)
    n = 2 * STEPS
    dma = pltpu.SemaphoreType.DMA
    return pl.pallas_call(
        reduce_kernel,
        out_shape=[
            jax.ShapeDtypeStruct((OUT // 64, IN), F32),
            jax.ShapeDtypeStruct((4, 2, IN // 64, IN), BF),
            jax.ShapeDtypeStruct((4, 2, OUT // 64, OUT), BF),
        ],
        in_specs=[anyspace] * 4,
        out_specs=[anyspace] * 3,
        scratch_shapes=[
            pltpu.VMEM((HALF, 2 * TOK), BF),
            pltpu.VMEM((TOK, HALF), BF),
            pltpu.VMEM((2, TOK, 2 * W), BF),
            pltpu.VMEM((TOK, IN), BF),
            pltpu.VMEM((2, 2, 2, HALF, COLS), F32),
            pltpu.VMEM((2, 2, 2, 3, 4, SEG, COLS), BF),
            pltpu.VMEM((n, 2, 4, SEG, COLS), BF),
            pltpu.VMEM((n, 2, 2, 4, SEG, COLS), BF),
            pltpu.VMEM((2, 4, SEG, COLS), F32),
            pltpu.VMEM((2, 4, SEG, COLS), BF),
            pltpu.VMEM((STEPS, 4, SEG, COLS), BF),
            pltpu.VMEM((2, 4, SEG, COLS), BF),
            pltpu.VMEM((STEPS, SEG, COLS), BF),
            pltpu.VMEM((STEPS, 2, SEG, COLS), BF),
            pltpu.VMEM((2, 2, 4, SEG, COLS), F32),
            pltpu.VMEM((2, 2, 3, SEG, COLS), BF),
            pltpu.VMEM((STEPS, 2, SEG, COLS), BF),
            pltpu.VMEM((STEPS, 2, 2, SEG, COLS), BF),
            pltpu.VMEM((2, 2, SEG, COLS), F32),
            pltpu.VMEM((2, SEG, COLS), F32),
            pltpu.VMEM((STEPS, SEG, COLS), F32),
            pltpu.VMEM((RZ, IN), BF),
            dma((2,)),
            dma((1 + STEPS,)),
            dma((1 + STEPS,)),
            dma((2, 2)),
            dma((n, 2)),
            dma((2, 2)),
            dma((n, 2)),
            dma((2, 2)),
            dma((n,)),
            dma((2, 2)),
            dma((n, 2)),
            dma((n,)),
            dma((n,)),
            dma((6,)),
            dma((6,)),
            dma((A_SLICES,)),
            dma((A_SLICES,)),
            dma((2,)),
            dma((2,)),
            dma((2, 2)),
            dma((2, 2)),
            dma((2,)),
            dma((8,)),
            dma((2,)),
            dma((4,)),
            pltpu.VMEM((2, 2, OUT // 64, OUT), BF),
            pltpu.VMEM((4, OUT, COLS), BF),
            pltpu.VMEM((OUT // 64, IN), F32),
            dma((4, 3)),
            dma((4, 3)),
            dma((4,)),
            dma((4,)),
            dma((4, 7)),
            dma((4, 7)),
        ],
        compiler_params=pltpu.CompilerParams(
            collective_id=0, has_side_effects=True, vmem_limit_bytes=63 * 1024 * 1024
        ),
        cost_estimate=pl.CostEstimate(flops=29_400_000_000, bytes_accessed=40_000_000, transcendentals=0),
        name="kfac_update",
    )(inputs, out_grad, a_inverse, g_inverse)


def per_device(inputs, out_grad, a_inverse, g_inverse, weights, momentum):
    update = reduce_call(inputs, out_grad, a_inverse, g_inverse)[0]
    new_momentum = 0.9 * momentum + update
    new_weights = weights - 0.5 * new_momentum
    return (new_weights, new_momentum)


def solution(mesh):
    spec = P(("pipe", "dp"), None)
    return jax.shard_map(
        per_device, mesh=mesh, in_specs=(spec,) * 6, out_specs=(spec, spec), check_vma=False
    )
```

```python
import functools

import jax
import jax.numpy as jnp
from jax import lax
from jax.experimental import pallas as pl
from jax.experimental.pallas import tpu as pltpu
from jax.sharding import PartitionSpec as P

BF = jnp.bfloat16
F32 = jnp.float32
MESH = pl.DeviceIdType.MESH
NZ, NY = 4, 4
IN, OUT, TOK = 4096, 4608, 640
HALF = OUT // 2
RZ = HALF // NZ
SEG = RZ // NY
W = 256
STEPS = IN // (2 * W)
COLS = 128
ROWHALF = (slice(0, 80), slice(80, 144))
LAST = STEPS + 6
G_PAIR, G_PACK = 11, 12
GK = OUT // 4
SLICE = 512
A_SLICES = IN // SLICE


def coords():
    d = lax.axis_index("dp")
    return d // 16, (d // 4) % 4, (d // 2) % 2, d % 2


def dev(z, y, x, c):
    return {"dp": ((z * 4 + y) * 2 + x) * 2 + c}


def remote(src, dst, ssem, rsem, to):
    return pltpu.make_async_remote_copy(
        src_ref=src, dst_ref=dst, send_sem=ssem, recv_sem=rsem, device_id=to, device_id_type=MESH
    )


def greet(peers):
    barrier = pltpu.get_barrier_semaphore()
    for p in peers:
        pl.semaphore_signal(barrier, inc=1, device_id=p, device_id_type=MESH)
    pl.semaphore_wait(barrier, len(peers))


def reduce_kernel(
    in_ref, og_ref, a_ref, g_ref, u_out, ag_hbm, gg_hbm,
    ogt, ogr, inb, inr, acc, s1, r1a, r1bc,
    sums0, mx, qx, m2, q2a, q2bc, sums, s2, r2a, r2bc, tot, sx, rx, xg,
    ld_sem, pair_s, pair_r, s1_sem, r1_sem, s2_sem, r2_sem, x_s, x_r, yg_s, yg_r, fw_s, fw_r, ag_s, ag_r, ra_s, ra_r, gp_s, gp_r, gf_s, gf_r, own_sem,
    al_sem, gl_sem, st_sem, gst, rg, uo, z_s, z_r, c_s, c_r, u_s, u_r,
):
    z, y, x, c = coords()
    core = dev(z, y, x, 1 - c)
    xpeer = dev(z, y, 1 - x, c)
    zs = [dev((z + k) % 4, y, x, c) for k in (1, 2, 3)]
    ys = [dev(z, (y + k) % 4, x, c) for k in (1, 2, 3)]
    offs = [(k, e) for k in range(4) for e in range(2) if (k, e) != (0, 0)]
    yx = [dev(z, (y + k) % 4, (x + e) % 2, c) for k, e in offs]
    greet([core] + zs + yx)
    my_rows = pl.ds(pl.multiple_of(c * HALF + z * RZ, 16), RZ)
    core_rows = pl.ds(pl.multiple_of(c * HALF, 16), HALF)
    other_rows = pl.ds(pl.multiple_of((1 - c) * HALF, 16), HALF)

    other = pl.multiple_of((1 - c) * HALF, 128)
    mine = pl.multiple_of(c * HALF, 128)

    og_x = remote(og_ref.at[:, pl.ds(other, HALF)], ogr, pair_s.at[0], pair_r.at[0], core)
    og_x.start()

    def in_x(s):
        cols = pl.ds(pl.multiple_of(s * 2 * W, 2 * W), 2 * W)
        return remote(in_ref.at[:, cols], inr.at[:, cols], pair_s.at[1 + s], pair_r.at[1 + s], core)

    in_x(0).start()

    def in_load(s):
        cols = pl.ds(pl.multiple_of(s * 2 * W, 2 * W), 2 * W)
        return pltpu.make_async_copy(in_ref.at[:, cols], inb.at[s % 2], ld_sem.at[s % 2])


    own_a = pltpu.make_async_copy(a_ref, ag_hbm.at[z, c], own_sem.at[0])
    own_g = pltpu.make_async_copy(g_ref, gg_hbm.at[y, x], own_sem.at[1])
    own_a.start()
    own_g.start()
    a_sends = [remote(a_ref, ag_hbm.at[z, c], ag_s.at[k], ag_r.at[k], zs[2 * k]) for k in range(2)]
    g_sends = [remote(g_ref, gg_hbm.at[y, x], ag_s.at[2 + k], ag_r.at[2 + k], ys[2 * k]) for k in range(2)]
    a_fwd = remote(ag_hbm.at[:, c], ag_hbm.at[:, c], ag_s.at[4], ag_r.at[4], core)
    g_own = remote(g_ref, gg_hbm.at[y, x], ag_s.at[5], ag_r.at[5], xpeer)
    for cp in a_sends + g_sends + [g_own]:
        cp.start()

    def relay(out, sem, i, k, other_k, axis, d):
        cols = pl.ds(pl.multiple_of(i * SLICE, SLICE), SLICE)
        from_k = (k + 3) % 4 if d == 0 else (k + 1) % 4
        here = out.at[from_k, other_k, :, cols]
        return remote(here, here, sem[0].at[i], sem[1].at[i], axis[2 * d])

    def relay_a(i, d):
        return relay(ag_hbm, (ra_s, ra_r), i, z, c, zs, d)

    def g_pair(d):
        here = gg_hbm.at[y, 1 - x]
        return remote(here, here, gp_s.at[d], gp_r.at[d], ys[2 * d])

    def g_far(e, d):
        half = OUT // 2
        here = gg_hbm.at[(y + 3 - 2 * d) % 4, e, :, d * half : (d + 1) * half]
        return remote(here, here, gf_s.at[e, d], gf_r.at[e, d], ys[2 * d])

    a_loads = [
        pltpu.make_async_copy(ag_hbm.at[i // 2, i % 2], inr.at[i * 64 : (i + 1) * 64], al_sem.at[i]) for i in range(8)
    ]

    def pack(k):
        there = (y + k) % 4
        cp = pltpu.make_async_copy(gg_hbm.at[there], gst.at[k % 2], gl_sem.at[k % 2])
        cp.start()
        cp.wait()
        for b in range(4):
            cols = slice(b * GK, (b + 1) * GK)
            v = jnp.concatenate([gst[k % 2, 0, :, cols], gst[k % 2, 1, :, cols]], axis=0)
            ogt[pl.ds(pl.multiple_of(b * RZ + there * SEG, 16), SEG), 0:GK] = v

    def between(s, lo, n):
        return jnp.logical_and(s >= lo, s < lo + n)

    def background(s):
        @pl.when(s == 1)
        def _():
            for cp in a_sends:
                cp.wait()

        @pl.when(s == G_PAIR)
        def _():
            g_own.wait()
            for d in range(2):
                g_pair(d).start()

        @pl.when(s == G_PACK)
        def _():
            own_g.wait()
            pack(0)

        @pl.when(between(s, 1, A_SLICES // 2))
        def _():
            relay_a(2 * (s - 1), 0).start()
            relay_a(2 * (s - 1) + 1, 1).start()

        @pl.when(between(s, 3, A_SLICES // 2))
        def _():
            relay_a(2 * (s - 3), 0).wait()
            relay_a(2 * (s - 3) + 1, 1).wait()

        @pl.when(s == 3 + A_SLICES // 2)
        def _():
            own_a.wait()
            a_fwd.start()

        @pl.when(s == 5 + A_SLICES // 2)
        def _():
            a_fwd.wait()
            for cp in a_loads:
                cp.start()

    part = HALF // 6

    def og_load(i):
        return pltpu.make_async_copy(
            og_ref.at[:, pl.ds(mine + i * part, part)], inb.at[i % 2, :, 0:part], ld_sem.at[i % 2]
        )

    og_load(0).start()
    for i in range(6):
        if i < 5:
            og_load(i + 1).start()
        og_load(i).wait()
        for j in range(part // 128):
            ogt[i * part + j * 128 : i * part + (j + 1) * 128, 0:TOK] = inb[i % 2, :, j * 128 : (j + 1) * 128].T
    in_load(0).start()
    og_x.wait()
    in_x(1).start()

    def turn_r(j, _):
        lanes = pl.ds(pl.multiple_of(j * 128, 128), 128)
        ogt[pl.ds(pl.multiple_of(j * 128, 128), 128), TOK : 2 * TOK] = ogr[:, lanes].T
        return 0

    lax.fori_loop(0, HALF // 128, turn_r, 0)

    first, second = (z, y), (y, z)
    stride1, stride2 = (RZ, SEG), (SEG, RZ)
    axis1, axis2 = (zs, ys), (ys, zs)

    def near(k, d):
        return (k + 1) % 4 if d == 0 else (k + 3) % 4

    def rows(t, k, j):
        return pl.ds(pl.multiple_of(k * stride1[t] + j * stride2[t], 16), SEG)

    def ch(s, t):
        return 2 * s + t

    def send_a(s, t, d):
        return remote(s1.at[t, s % 2, d, 0], r1a.at[ch(s, t), d], s1_sem.at[t, s % 2], r1_sem.at[ch(s, t), 0], axis1[t][2 * d])

    def send_bc(s, t, d):
        return remote(s1.at[t, s % 2, d, pl.ds(1, 2)], r1bc.at[ch(s, t), d], s1_sem.at[t, s % 2], r1_sem.at[ch(s, t), 1], axis1[t][2 * d])

    def send_half(s, t, d, h):
        return remote(s1.at[t, s % 2, d, 1 + h], r1bc.at[ch(s, t), d, h], s1_sem.at[t, s % 2], r1_sem.at[ch(s, t), 1], axis1[t][2 * d])

    def send_2a(s, t, d):
        if t == 0:
            half = ROWHALF[d]
            return remote(m2.at[s % 2, d, half], q2a.at[s, half], s2_sem.at[t, s % 2], r2_sem.at[ch(s, t), 0], axis2[t][2 * d])
        return remote(s2.at[s % 2, d, 0], r2a.at[s, d], s2_sem.at[t, s % 2], r2_sem.at[ch(s, t), 0], axis2[t][2 * d])

    def send_2bc(s, t, d):
        if t == 0:
            return remote(m2.at[s % 2, 2 + d], q2bc.at[s, d], s2_sem.at[t, s % 2], r2_sem.at[ch(s, t), 1], axis2[t][2 * d])
        return remote(s2.at[s % 2, d, pl.ds(1, 2)], r2bc.at[s, d], s2_sem.at[t, s % 2], r2_sem.at[ch(s, t), 1], axis2[t][2 * d])

    def far_2(s, t):
        if t == 0:
            return [remote(m2.at[s % 2, 0], q2a.at[s], s2_sem.at[t, s % 2], r2_sem.at[ch(s, t), 0], ys[1])]
        return [
            remote(s2.at[s % 2, d, 0], r2a.at[s, d], s2_sem.at[t, s % 2], r2_sem.at[ch(s, t), 0], zs[1]) for d in range(2)
        ]

    def far_y(s, t):
        here = xg.at[pl.ds(pl.multiple_of(y * SEG, 16), SEG), tile(s, t)]
        return remote(here, here, yg_s.at[t, s % 2], yg_r.at[ch(s, t), 1], ys[1])

    def at_last(s, f, g):
        pl.when(s == STEPS - 1)(f)
        pl.when(s < STEPS - 1)(g)

    def send_x(s, t):
        if t == 0:
            return remote(mx.at[s % 2], qx.at[s], x_s.at[t, s % 2], x_r.at[ch(s, t)], xpeer)
        return remote(sx.at[s % 2], rx.at[s], x_s.at[t, s % 2], x_r.at[ch(s, t)], xpeer)

    def tile(s, t):
        return pl.ds(pl.multiple_of(ch(s, t) * W + x * COLS, COLS), COLS)

    def send_y(s, t, d):
        here = xg.at[pl.ds(pl.multiple_of(y * SEG, 16), SEG), tile(s, t)]
        return remote(here, here, yg_s.at[t, s % 2], yg_r.at[ch(s, t), 0], ys[2 * d])

    def relay_y(s, t):
        behind = near(y, 1 - t)
        here = xg.at[pl.ds(pl.multiple_of(behind * SEG, 16), SEG), tile(s, t)]
        return remote(here, here, yg_s.at[t, s % 2], yg_r.at[ch(s, t), 1], ys[2 * t])

    def send_fw(s, t, k):
        here = xg.at[pl.ds(pl.multiple_of((y + k) % 4 * SEG, 16), SEG), tile(s, t)]
        return remote(here, here, fw_s.at[ch(s, t)], fw_r.at[ch(s, t)], xpeer)

    def arrived(ref, sem):
        pltpu.make_async_copy(ref, ref, sem).wait()

    def fetch(s):
        in_load(s).wait()
        in_x(s).wait()

        @pl.when(s + 1 < STEPS)
        def _():
            in_load(s + 1).start()

        @pl.when(s + 2 < STEPS)
        def _():
            in_x(s + 2).start()

    def compute(s, ts):
        p = s % 2
        for t in ts:
            b_own = inb[p, :, t * W : (t + 1) * W]
            b_other = inr[:, pl.ds(pl.multiple_of(ch(s, t) * W, W), W)]

            def block(i, _):
                r = pl.ds(pl.multiple_of(i * RZ, 16), RZ)
                v = jnp.dot(ogt[r, 0:TOK], b_own, preferred_element_type=F32)
                v = v + jnp.dot(ogt[r, TOK : 2 * TOK], b_other, preferred_element_type=F32)
                acc[t, p, 0, r, :] = v[:, :COLS]
                acc[t, p, 1, r, :] = v[:, COLS:]
                return 0

            lax.fori_loop(0, NZ, block, 0)

    def send_first(s, t):
        p, m = s % 2, first[t]
        for d in range(2):
            for j in range(4):
                s1[t, p, d, 0, j] = acc[t, p, d, rows(t, (m + 2) % 4, j), :].astype(BF)
            send_a(s, t, d).start()
        for d in range(2):
            for j in range(4):
                s1[t, p, d, 2 - d, j] = acc[t, p, 1 - d, rows(t, near(m, d), j), :].astype(BF)

            @pl.when(s == STEPS - 1)
            def _(d=d):
                send_half(s, t, d, 1 - d).start()

    def pass_on(s, t):
        p = s % 2
        arrived(r1a.at[ch(s, t)], r1_sem.at[ch(s, t), 0])
        for d in range(2):
            for j in range(4):
                v = acc[t, p, d, rows(t, near(first[t], d), j), :] + r1a[ch(s, t), d, j].astype(F32)
                s1[t, p, d, 1 + d, j] = v.astype(BF)

            @pl.when(s == STEPS - 1)
            def _(d=d):
                send_half(s, t, d, d).start()

            @pl.when(s < STEPS - 1)
            def _(d=d):
                send_bc(s, t, d).start()

    def sum_first0(s):
        p = s % 2
        arrived(r1bc.at[ch(s, 0)], r1_sem.at[ch(s, 0), 1])

        def summed(h, j):
            v = acc[0, p, h, rows(0, z, j), :]
            return v + r1bc[ch(s, 0), 0, h, j].astype(F32) + r1bc[ch(s, 0), 1, h, j].astype(F32)

        for j in range(4):
            mx[p, j] = summed(1 - x, j).astype(BF)
        send_x(s, 0).start()
        for j in range(4):
            sums0[p, j] = summed(x, j)
        arrived(s1.at[0, p], s1_sem.at[0, p])

    def second0(s):
        p = s % 2
        send_x(s, 0).wait()
        for j in range(4):
            sums0[p, j] = sums0[p, j] + qx[s, j].astype(F32)
        far = sums0[p, (y + 2) % 4].astype(BF)
        for d in range(2):
            m2[p, d] = far

        def direct():
            for d in range(2):
                m2[p, 2 + d] = sums0[p, near(y, d)].astype(BF)
                send_2bc(s, 0, d).start()
            for cp in far_2(s, 0):
                cp.start()

        def relayed():
            for d in range(2):
                send_2a(s, 0, d).start()
            for d in range(2):
                half = ROWHALF[1 - d]
                m2[p, 2 + d, half, :] = sums0[p, near(y, d), half, :].astype(BF)

        at_last(s, direct, relayed)

    def pass_on_second0(s):
        p = s % 2
        arrived(q2a.at[s], r2_sem.at[ch(s, 0), 0])

        @pl.when(s < STEPS - 1)
        def _():
            for d in range(2):
                half = ROWHALF[d]
                v = sums0[p, near(y, d), half, :] + q2a[s, half, :].astype(F32)
                m2[p, 2 + d, half, :] = v.astype(BF)
                send_2bc(s, 0, d).start()

    def finish0(s):
        p = s % 2
        arrived(q2bc.at[s], r2_sem.at[ch(s, 0), 1])
        v = sums0[p, y] + q2bc[s, 0].astype(F32) + q2bc[s, 1].astype(F32)
        v = v + jnp.where(s == STEPS - 1, q2a[s].astype(F32), 0.0)
        xg[pl.ds(pl.multiple_of(y * SEG, 16), SEG), tile(s, 0)] = v.astype(BF)
        for d in range(2):
            send_y(s, 0, d).start()
        send_fw(s, 0, 0).start()
        pl.when(s == STEPS - 1)(lambda: far_y(s, 0).start())
        arrived(m2.at[p, pl.ds(1, 3)], s2_sem.at[0, p])

    def sum_first1(s):
        t, p, m = 1, s % 2, z
        arrived(r1bc.at[ch(s, t)], r1_sem.at[ch(s, t), 1])
        for h in range(2):
            for j in range(4):
                v = acc[t, p, h, rows(t, y, j), :]
                sums[p, h, j] = v + r1bc[ch(s, t), 0, h, j].astype(F32) + r1bc[ch(s, t), 1, h, j].astype(F32)
        for d in range(2):
            s2[p, d, 0] = sums[p, d, (m + 2) % 4].astype(BF)
        for d in range(2):
            s2[p, d, 2 - d] = sums[p, 1 - d, near(m, d)].astype(BF)

        def direct():
            for d in range(2):
                s2[p, d, 1 + d] = sums[p, d, near(m, d)].astype(BF)
                send_2bc(s, t, d).start()
            for cp in far_2(s, t):
                cp.start()

        def relayed():
            for d in range(2):
                send_2a(s, t, d).start()

        at_last(s, direct, relayed)
        arrived(s1.at[t, p], s1_sem.at[t, p])

    def pass_on_second1(s):
        p = s % 2
        arrived(r2a.at[s], r2_sem.at[ch(s, 1), 0])

        @pl.when(s < STEPS - 1)
        def _():
            for d in range(2):
                v = sums[p, d, near(z, d)] + r2a[s, d].astype(F32)
                s2[p, d, 1 + d] = v.astype(BF)
                send_2bc(s, 1, d).start()

    def sum_second1(s):
        p = s % 2
        arrived(r2bc.at[s], r2_sem.at[ch(s, 1), 1])
        for h in range(2):
            v = sums[p, h, z] + r2bc[s, 0, h].astype(F32) + r2bc[s, 1, h].astype(F32)
            tot[p, h] = v + jnp.where(s == STEPS - 1, r2a[s, h].astype(F32), 0.0)
        sx[p] = tot[p, 1 - x]
        send_x(s, 1).start()
        arrived(s2.at[p], s2_sem.at[1, p])

    def finish1(s):
        send_x(s, 1).wait()
        v = tot[s % 2, x] + rx[s]
        xg[pl.ds(pl.multiple_of(y * SEG, 16), SEG), tile(s, 1)] = v.astype(BF)
        for d in range(2):
            send_y(s, 1, d).start()
        send_fw(s, 1, 0).start()
        pl.when(s == STEPS - 1)(lambda: far_y(s, 1).start())

    def relay_tiles(s, t):
        arrived(xg.at[pl.ds(0, 2 * SEG), tile(s, t)], yg_r.at[ch(s, t), 0])
        pl.when(s < STEPS - 1)(lambda: relay_y(s, t).start())
        send_fw(s, t, 1).start()
        send_fw(s, t, 3).start()

    def forward(s, t):
        arrived(xg.at[pl.ds(0, SEG), tile(s, t)], yg_r.at[ch(s, t), 1])
        send_fw(s, t, 2).start()
        arrived(xg.at[pl.ds(0, 3 * SEG), tile(s, t)], yg_s.at[t, s % 2])

    def complete(s, t):
        whole = xg.at[:, tile(s, t)]
        arrived(whole, fw_s.at[ch(s, t)])
        arrived(whole, fw_r.at[ch(s, t)])

    def both(f):
        def g(s):
            for t in range(2):
                f(s, t)

        return g

    stages = [
        (2, sum_first0),
        (2, sum_first1),
        (1, both(pass_on)),
        (3, pass_on_second0),
        (3, sum_second1),
        (4, both(relay_tiles)),
        (0, fetch),
        (0, lambda s: compute(s, (0,))),
        (2, pass_on_second1),
        (0, lambda s: send_first(s, 0)),
        (0, lambda s: compute(s, (1,))),
        (0, lambda s: send_first(s, 1)),
        (2, second0),
        (3, finish1),
        (3, finish0),
        (6, both(complete)),
        (4, both(forward)),
    ]

    def step(s, _):
        for lag, stage in stages:

            @pl.when(jnp.logical_and(s >= lag, s < STEPS + lag))
            def _(lag=lag, stage=stage):
                stage(s - lag)

        background(s)
        return 0

    lax.fori_loop(0, LAST, step, 0)
    for cp in a_loads:
        cp.wait()

    def send_r(q, d):
        here = rg.at[q, my_rows]
        return remote(here, here, z_s.at[q, d], z_r.at[q, d], zs[2 * d])

    def relay_r(q):
        d = q % 2
        behind = near(z, 1 - d)
        here = rg.at[q, pl.ds(pl.multiple_of(c * HALF + behind * RZ, 16), RZ)]
        return remote(here, here, z_s.at[q, 2], z_r.at[q, 2], zs[2 * d])

    def send_core(q, k):
        here = rg.at[q, pl.ds(pl.multiple_of(c * HALF + ((z + k) % 4) * RZ, 16), RZ)]
        return remote(here, here, c_s.at[q], c_r.at[q], core)

    def utile(q):
        return pl.ds(pl.multiple_of(((q * 4 + y) * 2 + x) * COLS, COLS), COLS)

    def urows(owner):
        return pl.ds(pl.multiple_of(owner * (OUT // 64), 8), OUT // 64)

    def send_u(q, i):
        k, e = offs[i]
        owner = ((y + k) % 4) * 2 + (x + e) % 2
        return remote(acc.at[q // 2, q % 2, 0, urows(owner)], uo.at[:, utile(q)], u_s.at[q, i], u_r.at[q, i], yx[i])

    def right(q):
        v = lax.dot_general(
            xg[...], inr[q * COLS : (q + 1) * COLS, :], (((1,), (1,)), ((), ())), preferred_element_type=F32
        )
        rg[q, my_rows, :] = v.astype(BF)
        for d in range(2):
            send_r(q, d).start()
        send_core(q, 0).start()

    def pass_right(q):
        for d in range(2):
            send_r(q, d).wait()
        relay_r(q).start()
        send_core(q, 1).start()
        send_core(q, 3).start()

    def share_right(q):
        relay_r(q).wait()
        send_core(q, 2).start()

    def update(q):
        arrived(rg.at[q, core_rows], c_s.at[q])
        arrived(rg.at[q, other_rows], c_r.at[q])
        v = jnp.zeros((RZ, COLS), F32)
        for b in range(4):
            v = v + jnp.dot(
                ogt[b * RZ : (b + 1) * RZ, 0:GK], rg[q, b * GK : (b + 1) * GK, :], preferred_element_type=F32
            )
        acc[q // 2, q % 2, 0, 0:RZ, :] = v
        uo[:, utile(q)] = acc[q // 2, q % 2, 0, urows(y * 2 + x), :]
        for i in range(7):
            send_u(q, i).start()

    right(0)
    right(1)
    for cp in g_sends:
        cp.wait()
    for d in range(2):
        g_pair(d).wait()
    for e in range(2):
        for d in range(2):
            g_far(e, d).start()
    pass_right(0)
    right(2)
    pass_right(1)
    pack(1)
    right(3)
    share_right(0)
    pass_right(2)
    pack(3)
    share_right(1)
    pass_right(3)
    for e in range(2):
        for d in range(2):
            g_far(e, d).wait()
    pack(2)
    update(0)
    share_right(2)
    update(1)
    share_right(3)
    update(2)
    update(3)
    def store(q):
        cols = pl.ds(q * 8 * COLS, 8 * COLS)
        return pltpu.make_async_copy(uo.at[:, cols], u_out.at[:, cols], st_sem.at[q])

    for q in range(4):
        for i in range(7):
            send_u(q, i).wait()
        store(q).start()
    for q in range(4):
        store(q).wait()


def reduce_call(inputs, out_grad, a_inverse, g_inverse):
    anyspace = pl.BlockSpec(memory_space=pl.ANY)
    n = 2 * STEPS
    dma = pltpu.SemaphoreType.DMA
    return pl.pallas_call(
        reduce_kernel,
        out_shape=[
            jax.ShapeDtypeStruct((OUT // 64, IN), F32),
            jax.ShapeDtypeStruct((4, 2, IN // 64, IN), BF),
            jax.ShapeDtypeStruct((4, 2, OUT // 64, OUT), BF),
        ],
        in_specs=[anyspace] * 4,
        out_specs=[anyspace] * 3,
        scratch_shapes=[
            pltpu.VMEM((HALF, 2 * TOK), BF),
            pltpu.VMEM((TOK, HALF), BF),
            pltpu.VMEM((2, TOK, 2 * W), BF),
            pltpu.VMEM((TOK, IN), BF),
            pltpu.VMEM((2, 2, 2, HALF, COLS), F32),
            pltpu.VMEM((2, 2, 2, 3, 4, SEG, COLS), BF),
            pltpu.VMEM((n, 2, 4, SEG, COLS), BF),
            pltpu.VMEM((n, 2, 2, 4, SEG, COLS), BF),
            pltpu.VMEM((2, 4, SEG, COLS), F32),
            pltpu.VMEM((2, 4, SEG, COLS), BF),
            pltpu.VMEM((STEPS, 4, SEG, COLS), BF),
            pltpu.VMEM((2, 4, SEG, COLS), BF),
            pltpu.VMEM((STEPS, SEG, COLS), BF),
            pltpu.VMEM((STEPS, 2, SEG, COLS), BF),
            pltpu.VMEM((2, 2, 4, SEG, COLS), F32),
            pltpu.VMEM((2, 2, 3, SEG, COLS), BF),
            pltpu.VMEM((STEPS, 2, SEG, COLS), BF),
            pltpu.VMEM((STEPS, 2, 2, SEG, COLS), BF),
            pltpu.VMEM((2, 2, SEG, COLS), F32),
            pltpu.VMEM((2, SEG, COLS), F32),
            pltpu.VMEM((STEPS, SEG, COLS), F32),
            pltpu.VMEM((RZ, IN), BF),
            dma((2,)),
            dma((1 + STEPS,)),
            dma((1 + STEPS,)),
            dma((2, 2)),
            dma((n, 2)),
            dma((2, 2)),
            dma((n, 2)),
            dma((2, 2)),
            dma((n,)),
            dma((2, 2)),
            dma((n, 2)),
            dma((n,)),
            dma((n,)),
            dma((6,)),
            dma((6,)),
            dma((A_SLICES,)),
            dma((A_SLICES,)),
            dma((2,)),
            dma((2,)),
            dma((2, 2)),
            dma((2, 2)),
            dma((2,)),
            dma((8,)),
            dma((2,)),
            dma((4,)),
            pltpu.VMEM((2, 2, OUT // 64, OUT), BF),
            pltpu.VMEM((4, OUT, COLS), BF),
            pltpu.VMEM((OUT // 64, IN), F32),
            dma((4, 3)),
            dma((4, 3)),
            dma((4,)),
            dma((4,)),
            dma((4, 7)),
            dma((4, 7)),
        ],
        compiler_params=pltpu.CompilerParams(
            collective_id=0, has_side_effects=True, vmem_limit_bytes=63 * 1024 * 1024
        ),
        cost_estimate=pl.CostEstimate(flops=29_400_000_000, bytes_accessed=40_000_000, transcendentals=0),
        name="kfac_update",
    )(inputs, out_grad, a_inverse, g_inverse)


def per_device(inputs, out_grad, a_inverse, g_inverse, weights, momentum):
    update = reduce_call(inputs, out_grad, a_inverse, g_inverse)[0]
    new_momentum = 0.9 * momentum + update
    new_weights = weights - 0.5 * new_momentum
    return (new_weights, new_momentum)


def solution(mesh):
    spec = P(("pipe", "dp"), None)
    return jax.shard_map(
        per_device, mesh=mesh, in_specs=(spec,) * 6, out_specs=(spec, spec), check_vma=False
    )
```
